128 devices in a mesh: rows: 16 (over x, z), rep: 8 (over y, core).
Axes of the slice: x: 4, y: 4, z: 4, core: 2. Of those that a mesh axis runs over, the one named last changes fastest.
Arguments:
- features: bfloat16 [131072, 256], P(('rows', 'rep')), may hold values from -6 to 6
- weight: bfloat16 [256, 256], replicated, may hold values from -0.375 to 0.375
- tile_values: bfloat16 [1024, 48, 128, 128], P(('rows', 'rep')), may hold values from -0.125 to 0.125
- tile_cols: int32 [1024, 48], P(('rows', 'rep')), may hold values from 0 to 1023, as said below
- tile_live: int32 [1024, 48], P(('rows', 'rep')), may hold values from 0 to 1, as said below
- cotangent: bfloat16 [131072, 256], P(('rows', 'rep')), may hold values from -6 to 6
Outputs:
- output: bfloat16 [131072, 256], P(('rows', 'rep'))
- feature_grad: bfloat16 [131072, 256], P(('rows', 'rep'))
- weight_grad: float32 [256, 256], replicated
The draws below stay inside these ranges and needn't reach their ends.
Inputs may be any that keep to these rules, and one draw needn't show every extreme that they name: `tile_cols`: row tile t names only column tiles of node groups g - 1, g and g + 1 modulo 16, where g = t // 64 and group k holds column tiles k * 64 to (k + 1) * 64 - 1; a column tile may repeat. `tile_live`: the live slots of each row tile come first; every row tile has at least one; row tiles whose index is a multiple of 8 have all 48 live.
All inputs are finite; a program needn't handle non-finite values.
Results may differ from the reference program's by a relative error of at most 0.02.
Values may be sent and summed in bfloat16 or wider, within the bound.
No kernel may reach another device: no remote copies, remote signals or barrier semaphores. Data moves between devices by JAX's collectives and lax.ppermute only.
A program may use at most 192 MiB of HBM per device.

```python
import jax
import jax.numpy as jnp
from jax import lax

F = 256
TILE = 128
SLOTS = 48
GROUPS = 16
GROUP_TILES = 64
ROWT = 8
NODES = 131072
ROW_TILES = 1024


def draw_tile_cols(key, part):
    first, second = jax.random.split(jax.random.fold_in(key, 11))
    rowidx = jnp.arange(ROW_TILES, dtype=jnp.int32)[:, None]
    group = rowidx // GROUP_TILES
    offset = jax.random.randint(first, (ROW_TILES, SLOTS), -1, 2, dtype=jnp.int32)
    inner = jax.random.randint(second, (ROW_TILES, SLOTS), 0, GROUP_TILES, dtype=jnp.int32)
    return (jnp.mod(group + offset, GROUPS) * GROUP_TILES + inner).astype(jnp.int32)


def draw_tile_live(key, part):
    first, second = jax.random.split(jax.random.fold_in(key, 23))
    loads = jax.random.randint(first, (ROW_TILES,), 1, SLOTS + 1, dtype=jnp.int32)
    scales = jax.random.randint(second, (ROW_TILES // ROWT,), 1, 5, dtype=jnp.int32)
    scales = jnp.repeat(scales, ROWT)
    counts = jnp.maximum(1, loads * scales // 4)
    rowidx = jnp.arange(ROW_TILES, dtype=jnp.int32)
    counts = jnp.where(rowidx % ROWT == 0, SLOTS, counts)
    slotidx = jnp.arange(SLOTS, dtype=jnp.int32)[None, :]
    return (slotidx < counts[:, None]).astype(jnp.int32)


def block_scale(own_key, dims, cuts, low, top_value):
    gain, own = 1.0, jax.random.fold_in(own_key, 6)
    for axis_at, shards_of in cuts:
        heights = jnp.exp(jax.random.uniform(jax.random.fold_in(own, axis_at), (shards_of,), jnp.float32, low / len(cuts), top_value / len(cuts)))
        gain = gain * jnp.repeat(heights, dims[axis_at] // shards_of).reshape([-1 if axis == axis_at else 1 for axis in range(len(dims))])
    return gain


def gaussian(stream_key, dims, width, bound, cuts=(), held_as=jnp.bfloat16):
    values = jax.random.normal(stream_key, dims, jnp.float32) * width
    if len(cuts) > 0:
        values = block_scale(stream_key, dims, cuts, -0.22, 0.18) * values
    return jnp.clip(values, min=-bound, max=bound).astype(held_as)


def setup_inputs(seed: int = 0) -> dict:
    arg_keys = jax.random.split(jax.random.key(seed), 7)
    features = gaussian(arg_keys[0], (NODES, F), 1.0, 6.0, ((0, 128),))
    weight = gaussian(arg_keys[1], (F, F), F ** -0.5, 0.375)
    tile_values = gaussian(arg_keys[2], (ROW_TILES, SLOTS, TILE, TILE), (TILE * SLOTS // 3) ** -0.5, 0.125, ((0, 128),))
    tile_cols = draw_tile_cols(jax.random.fold_in(arg_keys[6], 71), 0)
    tile_live = draw_tile_live(jax.random.fold_in(arg_keys[6], 71), 0)
    cotangent = gaussian(arg_keys[5], (NODES, F), 1.0, 6.0, ((0, 128),))
    return dict(features=features, weight=weight, tile_values=tile_values, tile_cols=tile_cols, tile_live=tile_live, cotangent=cotangent)


def reference(features, weight, tile_values, tile_cols, tile_live, cotangent):
    hidden = jnp.dot(features, weight, preferred_element_type=jnp.float32).astype(jnp.bfloat16)
    hid_tiles = hidden.reshape(ROW_TILES, TILE, F)

    def forward_row(item):
        values, columns, live = item
        chosen = hid_tiles[columns]
        masked = values * live.astype(jnp.bfloat16)[:, None, None]
        return jnp.einsum("sij,sjf->if", masked.astype(jnp.float32), chosen.astype(jnp.float32))

    pre = lax.map(forward_row, (tile_values, tile_cols, tile_live)).reshape(NODES, F)
    sig = jax.nn.sigmoid(pre)
    output = (pre * sig).astype(jnp.bfloat16)
    grad_pre = (cotangent.astype(jnp.float32) * sig * (1.0 + pre * (1.0 - sig))).astype(jnp.bfloat16)
    grad_tiles = grad_pre.reshape(ROW_TILES, TILE, F)

    def backward_row(accum, item):
        values, columns, live, grads = item
        masked = values * live.astype(jnp.bfloat16)[:, None, None]
        contrib = jnp.einsum("sij,if->sjf", masked.astype(jnp.float32), grads.astype(jnp.float32))
        return accum.at[columns].add(contrib), None

    start = jnp.zeros((ROW_TILES, TILE, F), jnp.float32)
    accum, _ = lax.scan(backward_row, start, (tile_values, tile_cols, tile_live, grad_tiles))
    grad_hidden = accum.reshape(NODES, F).astype(jnp.bfloat16)
    feature_grad = jnp.dot(grad_hidden, weight.T, preferred_element_type=jnp.float32).astype(jnp.bfloat16)
    weight_grad = jnp.dot(features.T, grad_hidden, preferred_element_type=jnp.float32)
    return (output, feature_grad, weight_grad)
```

```python
import jax, jax.numpy as jnp
from jax import lax
from jax.experimental import pallas as pl
from jax.experimental.pallas import tpu as pltpu
from jax.sharding import PartitionSpec as P

bf16, f32 = jnp.bfloat16, jnp.float32
U = 4

def pairs(a_ref, t_n, k0):
    tiles = []
    for u in range(U):
        a = a_ref[0, k0 + u]
        tiles.append(jnp.where(k0 + u < t_n, a, jnp.zeros_like(a)))
    return [jnp.concatenate(tiles[u:u+2], axis=1) for u in range(0, U, 2)]

def kernel(idx, cnt, a_ref, win_ref, w_ref, cot_ref, out_ref, wg_ref, grad_hbm, acc, stage, sem):
    t = pl.program_id(0)
    nt = pl.num_programs(0)
    n_win = acc.shape[0]
    @pl.when(t == 0)
    def _():
        wg_ref[...] = jnp.zeros_like(wg_ref)
        def zero(i, _):
            acc[i] = jnp.zeros(acc.shape[1:], f32)
            return 0
        lax.fori_loop(0, n_win, zero, 0)
    n = cnt[t]
    trips = (n + U - 1) // U
    def fwd(i, af):
        k0 = i * U
        for p, a in enumerate(pairs(a_ref, n, k0)):
            w = jnp.concatenate([win_ref[pl.ds(pl.multiple_of(idx[t, k0 + 2*p + u] * 128, 128), 128), :] for u in range(2)], axis=0)
            af = af + jnp.dot(a, w, preferred_element_type=f32)
        return af
    af = lax.fori_loop(0, trips, fwd, jnp.zeros((128, 256), f32))
    afb = af.astype(bf16)
    pre = jnp.dot(afb, w_ref[...], preferred_element_type=f32)
    sig = jax.nn.sigmoid(pre)
    out_ref[...] = (pre * sig).astype(bf16)
    g = (cot_ref[...].astype(f32) * sig * (1.0 + pre * (1.0 - sig))).astype(bf16)
    wg_ref[...] += lax.dot_general(afb, g, (((0,), (0,)), ((), ())), preferred_element_type=f32)
    gwt = lax.dot_general(w_ref[...], g, (((1,), (1,)), ((), ())), preferred_element_type=f32).astype(bf16)
    def bwd(i, _):
        k0 = i * U
        for p, a in enumerate(pairs(a_ref, n, k0)):
            r = jnp.dot(gwt, a, preferred_element_type=f32)
            for u in range(2):
                c = idx[t, k0 + 2*p + u]
                acc[c] += r[:, u*128:(u+1)*128]
        return 0
    lax.fori_loop(0, trips, bwd, 0)
    @pl.when(t == nt - 1)
    def _():
        per = stage.shape[1]
        steps = n_win // per
        def copy(i):
            return pltpu.make_async_copy(stage.at[i % 2], grad_hbm.at[pl.ds(i * per, per)], sem.at[i % 2])
        def emit(i, _):
            @pl.when(i >= 2)
            def _():
                copy(i - 2).wait()
            stage[i % 2] = acc[pl.ds(i * per, per)].astype(bf16)
            copy(i).start()
            return 0
        lax.fori_loop(0, steps, emit, 0)
        copy(steps - 2).wait()
        copy(steps - 1).wait()

def layer(idx, cnt, tile_values, win, weight, cotangent):
    nt, slots, tile, _ = tile_values.shape
    width = weight.shape[0]
    n_win = win.shape[0] // tile
    whole = lambda *s: pl.BlockSpec(s, lambda t, *_: (0,) * len(s), pipeline_mode=pl.Buffered(1))
    return pl.pallas_call(
        kernel,
        grid_spec=pltpu.PrefetchScalarGridSpec(
            num_scalar_prefetch=2, grid=(nt,),
            in_specs=[pl.BlockSpec((1, slots, tile, tile), lambda t, *_: (t, 0, 0, 0)),
                      whole(*win.shape), whole(width, width),
                      pl.BlockSpec((tile, width), lambda t, *_: (t, 0))],
            out_specs=[pl.BlockSpec((tile, width), lambda t, *_: (t, 0)),
                       pl.BlockSpec((width, width), lambda t, *_: (0, 0)),
                       pl.BlockSpec(memory_space=pl.ANY)],
            scratch_shapes=[pltpu.VMEM((n_win, width, tile), f32), pltpu.VMEM((2, 8, width, tile), bf16), pltpu.SemaphoreType.DMA((2,))]),
        out_shape=[jax.ShapeDtypeStruct((nt*tile, width), bf16), jax.ShapeDtypeStruct((width, width), f32),
                   jax.ShapeDtypeStruct((n_win, width, tile), bf16)],
        compiler_params=pltpu.CompilerParams(vmem_limit_bytes=60*2**20),
    )(idx, cnt, tile_values, win, weight, cotangent)


def ring(count, step):
    return [(i, (i + step) % count) for i in range(count)]


def weight_sum(term, n_rows, n_rep):
    rep = lax.axis_index("rep")
    height = term.shape[0] // n_rep
    pieces = term.reshape(n_rep, height, term.shape[1])

    def piece(at):
        return lax.dynamic_index_in_dim(pieces, jnp.mod(at, n_rep), 0, keepdims=False)

    own = piece(rep)
    for step in range(1, n_rep):
        own = own + lax.ppermute(piece(rep + step), "rep", ring(n_rep, step))
    part = 4
    for inner in (True, False):
        got = own
        for step in range(1, part):
            if inner:
                route = [(r, r // part * part + (r % part + step) % part) for r in range(n_rows)]
            else:
                route = [(r, (r + step * part) % n_rows) for r in range(n_rows)]
            got = got + lax.ppermute(own, "rows", route)
        own = got
    blocks = jnp.zeros_like(pieces)
    blocks = lax.dynamic_update_index_in_dim(blocks, own, rep, 0)
    for step in range(1, n_rep):
        got = lax.ppermute(own, "rep", ring(n_rep, step))
        blocks = lax.dynamic_update_index_in_dim(blocks, got, jnp.mod(rep - step, n_rep), 0)
    return blocks.reshape(term.shape)


def local(features, weight, tile_values, tile_cols, tile_live, cotangent):
    n_rows = lax.axis_size("rows")
    n_rep = lax.axis_size("rep")
    row_group = lax.axis_index("rows")
    node_dev, width = features.shape
    tile = tile_values.shape[2]
    own_tiles = node_dev // tile
    group_tiles = own_tiles * n_rep
    place = jnp.mod(tile_cols // group_tiles - row_group + 1, n_rows)
    inner = tile_cols % group_tiles
    idx = ((inner // own_tiles) * 3 + place) * own_tiles + inner % own_tiles
    cnt = jnp.sum(tile_live, axis=1)
    low = lax.ppermute(features, "rows", ring(n_rows, 1))
    high = lax.ppermute(features, "rows", ring(n_rows, -1))
    win = lax.all_gather(jnp.concatenate([low, features, high]), "rep", axis=0, tiled=True)
    output, term, grads = layer(idx, cnt, tile_values, win, weight, cotangent)
    weight_grad = weight_sum(term, n_rows, n_rep)
    grads = lax.psum_scatter(grads, "rep", scatter_dimension=0, tiled=True)
    down, mid, up = (grads[i * own_tiles : (i + 1) * own_tiles] for i in range(3))
    from_high = lax.ppermute(down, "rows", ring(n_rows, -1))
    from_low = lax.ppermute(up, "rows", ring(n_rows, 1))
    total = mid.astype(f32) + from_high.astype(f32) + from_low.astype(f32)
    feature_grad = jnp.swapaxes(total, 1, 2).reshape(node_dev, width).astype(bf16)
    return (output, feature_grad, weight_grad)


def solution(mesh):
    placed = (
        P(("rows", "rep"), None),
        P(),
        P(("rows", "rep"), None, None, None),
        P(("rows", "rep"), None),
        P(("rows", "rep"), None),
        P(("rows", "rep"), None),
    )
    return jax.shard_map(
        local,
        mesh=mesh,
        in_specs=placed,
        out_specs=(P(("rows", "rep"), None), P(("rows", "rep"), None), P()),
        check_vma=False,
    )
```

```python
import functools
import math

import jax
import jax.numpy as jnp
import numpy as np
from jax import lax
from jax.experimental import pallas as pl
from jax.experimental.pallas import tpu as pltpu
from jax.sharding import PartitionSpec as P

bf16, f32 = jnp.bfloat16, jnp.float32

CROSS = 4
FWD_SLOTS = 12
BWD_SLOTS = 8
STAGES = 4


def pieces_of(own):
    a = range(CROSS)
    b = range(CROSS, own)
    full = range(own)
    a2 = [(p, 2, i) for p in (1, 0, 2) for i in a]
    half = len(a2) // 2
    return [
        ("lz1", [(0, dy, i) for dy in (1, 3) for i in b]),
        ("lz2", [(0, 2, i) for i in b]),
        ("hz1", [(2, dy, i) for dy in (1, 3) for i in b]),
        ("hz2", [(2, 2, i) for i in b]),
        ("a2lo", a2[:half]),
        ("a2hi", a2[half:]),
        ("a1", [(p, 1, i) for p in (1, 0, 2) for i in a]),
        ("a3", [(p, 3, i) for p in (1, 0, 2) for i in a]),
        ("bb", [(1, dy, i) for dy in (1, 3) for i in b]),
        ("b2", [(1, 2, i) for i in b]),
        ("own", [(1, 0, i) for i in full]),
        ("low", [(0, 0, i) for i in full]),
        ("high", [(2, 0, i) for i in full]),
    ]


GROUPS = [
    ("lz1", "lz2"),
    ("hz1", "hz2"),
    ("a2lo", "a2hi"),
    ("a1", "a3"),
    ("bb", "b2"),
    ("own", "low", "high"),
]


def kernel(sizes, groups, chunk, idx, cnt, a_ref, *refs):
    n_in = 2 * len(sizes)
    n_out = 2 * len(groups)
    parts = refs[:n_in]
    w_ref, cot_ref, out_ref, wg_ref = refs[n_in : n_in + 4]
    outs = refs[n_in + 4 : n_in + 4 + n_out]
    win, acc, stage, in_sem, out_sem = refs[n_in + 4 + n_out :]
    t = pl.program_id(0)
    tile = a_ref.shape[2]

    @pl.when(t == 0)
    def _():
        copies, at = [], 0
        for k, part in enumerate(parts):
            rows = part.shape[0]
            copies.append(pltpu.make_async_copy(part, win.at[pl.ds(at, rows)], in_sem.at[k]))
            copies[-1].start()
            at += rows
        wg_ref[...] = jnp.zeros_like(wg_ref)

        def zero(i, _):
            acc[pl.ds(i * 4, 4)] = jnp.zeros((4,) + acc.shape[1:], f32)
            return 0

        lax.fori_loop(0, acc.shape[0] // 4, zero, 0)
        for copy in copies:
            copy.wait()

    n = cnt[t]

    def lanes(k0, count):
        got = []
        for j in range(count):
            a = a_ref[0, k0 + j]
            got.append(jnp.where(k0 + j < n, a, jnp.zeros_like(a)))
        return jnp.concatenate(got, axis=1)

    def forward(i, af):
        k0 = i * FWD_SLOTS
        rows = [
            win[pl.ds(pl.multiple_of(idx[t, k0 + j] * tile, tile), tile), :]
            for j in range(FWD_SLOTS)
        ]
        return af + jnp.dot(
            lanes(k0, FWD_SLOTS), jnp.concatenate(rows, axis=0), preferred_element_type=f32
        )

    width = w_ref.shape[0]
    trips = (n + FWD_SLOTS - 1) // FWD_SLOTS
    af = lax.fori_loop(0, trips, forward, jnp.zeros((tile, width), f32)).astype(bf16)
    pre = jnp.dot(af, w_ref[...], preferred_element_type=f32)
    sig = jax.nn.sigmoid(pre)
    out_ref[...] = (pre * sig).astype(bf16)
    g = (cot_ref[...].astype(f32) * sig * (1.0 + pre * (1.0 - sig))).astype(bf16)
    wg_ref[...] += lax.dot_general(af, g, (((0,), (0,)), ((), ())), preferred_element_type=f32)
    gwt = lax.dot_general(
        w_ref[...], g, (((1,), (1,)), ((), ())), preferred_element_type=f32
    ).astype(bf16)

    def backward(i, _):
        k0 = i * BWD_SLOTS
        r = jnp.dot(gwt, lanes(k0, BWD_SLOTS), preferred_element_type=f32)
        for j in range(BWD_SLOTS):
            acc[idx[t, k0 + j]] += r[:, j * tile : (j + 1) * tile]
        return 0

    lax.fori_loop(0, (n + BWD_SLOTS - 1) // BWD_SLOTS, backward, 0)

    @pl.when(t == pl.num_programs(0) - 1)
    def _():
        def copy(slot, out, at):
            return pltpu.make_async_copy(stage.at[slot], out.at[pl.ds(at, chunk)], out_sem.at[slot])

        done = 0
        for out in outs:
            steps = out.shape[0] // chunk

            def emit(i, _, out=out, done=done):
                number = done + i
                slot = lax.rem(number, STAGES)

                @pl.when(number >= STAGES)
                def _():
                    copy(slot, out, 0).wait()

                stage[slot] = acc[pl.ds(number * chunk, chunk)].astype(bf16)
                copy(slot, out, i * chunk).start()
                return 0

            lax.fori_loop(0, steps, emit, 0)
            done += steps
        for slot in range(STAGES):
            copy(slot, outs[0], 0).wait()


def layer(idx, cnt, tile_values, parts, weight, cotangent, sizes, groups):
    nt, slots, tile, _ = tile_values.shape
    width = weight.shape[0]
    n_win = 2 * sum(sizes)
    chunk = math.gcd(*groups)
    anywhere = pl.BlockSpec(memory_space=pl.ANY)
    return pl.pallas_call(
        functools.partial(kernel, sizes, groups, chunk),
        grid_spec=pltpu.PrefetchScalarGridSpec(
            num_scalar_prefetch=2,
            grid=(nt,),
            in_specs=[pl.BlockSpec((1, slots, tile, tile), lambda t, *_: (t, 0, 0, 0))]
            + [anywhere] * len(parts)
            + [
                pl.BlockSpec((width, width), lambda t, *_: (0, 0)),
                pl.BlockSpec((tile, width), lambda t, *_: (t, 0)),
            ],
            out_specs=[
                pl.BlockSpec((tile, width), lambda t, *_: (t, 0)),
                pl.BlockSpec((width, width), lambda t, *_: (0, 0)),
            ]
            + [anywhere] * (2 * len(groups)),
            scratch_shapes=[
                pltpu.VMEM((n_win * tile, width), bf16),
                pltpu.VMEM((n_win, width, tile), f32),
                pltpu.VMEM((STAGES, chunk, width, tile), bf16),
                pltpu.SemaphoreType.DMA((len(parts),)),
                pltpu.SemaphoreType.DMA((STAGES,)),
            ],
        ),
        out_shape=[
            jax.ShapeDtypeStruct((nt * tile, width), bf16),
            jax.ShapeDtypeStruct((width, width), f32),
        ]
        + [jax.ShapeDtypeStruct((g, width, tile), bf16) for _ in range(2) for g in groups],
        compiler_params=pltpu.CompilerParams(vmem_limit_bytes=60 * 2**20),
    )(idx, cnt, tile_values, *parts, weight, cotangent)


def ring(count, step):
    return [(i, (i + step) % count) for i in range(count)]


def from_z(x, step):
    return lax.ppermute(x, "rows", ring(lax.axis_size("rows"), -step))


def from_y(x, step):
    return lax.ppermute(x, "rep", ring(lax.axis_size("rep"), -2 * step))


def from_core(x):
    return lax.ppermute(x, "rep", [(i, i ^ 1) for i in range(lax.axis_size("rep"))])


def gather(features, tile, own):
    ha, hb = features[: CROSS * tile], features[CROSS * tile :]
    got = {"own": features}
    got["low"], got["high"] = from_z(features, -1), from_z(features, 1)
    b1, b3 = from_y(hb, 1), from_y(hb, -1)
    half = (own - CROSS) // 2 * tile
    got["bb"] = jnp.concatenate([b1, b3])
    got["lz1"], got["hz1"] = from_z(got["bb"], -1), from_z(got["bb"], 1)
    got["b2"] = jnp.concatenate([from_y(b1[:half], 1), from_y(b3[half:], -1)])
    got["lz2"], got["hz2"] = from_z(got["b2"], -1), from_z(got["b2"], 1)
    ycat = jnp.concatenate([ha, got["low"][: CROSS * tile], got["high"][: CROSS * tile]])
    got["a1"], got["a3"] = from_y(ycat, 1), from_y(ycat, -1)
    half = 3 * CROSS // 2 * tile
    got["a2lo"] = from_y(got["a1"][:half], 1)
    got["a2hi"] = from_y(got["a3"][half:], -1)
    return got


def scatter(mine, other, own):
    s = [m.astype(f32) + from_core(o).astype(f32) for m, o in zip(mine, other)]
    lz, hz, a2, a13, bb2, home = s
    nb = own - CROSS
    b = bb2 + from_z(lz.astype(bf16), 1).astype(f32) + from_z(hz.astype(bf16), -1).astype(f32)
    half, na = 3 * CROSS // 2, 3 * CROSS
    a2 = a2.astype(bf16)
    lo, hi = from_y(a2[:half], -1).astype(f32), from_y(a2[half:], 1).astype(f32)
    a1 = jnp.concatenate([a13[:half] + lo, a13[half:na]]).astype(bf16)
    a3 = jnp.concatenate([a13[na : na + half], a13[na + half :] + hi]).astype(bf16)
    ycat = from_y(a1, -1).astype(f32) + from_y(a3, 1).astype(f32)
    h, low, high = home[:own], home[own : 2 * own], home[2 * own :]
    ha = h[:CROSS] + ycat[:CROSS]
    low = jnp.concatenate([low[:CROSS] + ycat[CROSS : 2 * CROSS], low[CROSS:]]).astype(bf16)
    high = jnp.concatenate([high[:CROSS] + ycat[2 * CROSS :], high[CROSS:]]).astype(bf16)
    half = nb // 2
    b2 = b[2 * nb :].astype(bf16)
    lo, hi = from_y(b2[:half], -1).astype(f32), from_y(b2[half:], 1).astype(f32)
    b1 = jnp.concatenate([b[:half] + lo, b[half:nb]]).astype(bf16)
    b3 = jnp.concatenate([b[nb : nb + half], b[nb + half : 2 * nb] + hi]).astype(bf16)
    hb = h[CROSS:] + from_y(b1, -1).astype(f32) + from_y(b3, 1).astype(f32)
    return (
        jnp.concatenate([ha, hb]) + from_z(low, 1).astype(f32) + from_z(high, -1).astype(f32)
    )


def weight_sum(term, n_rows, n_rep):
    rep = lax.axis_index("rep")
    core, y = rep % 2, rep // 2
    n_y = n_rep // 2

    def piece(x, count, at):
        x = x.reshape(count, x.shape[0] // count, x.shape[1])
        return lax.dynamic_index_in_dim(x, jnp.mod(at, count), 0, keepdims=False)

    half = piece(term, 2, core) + from_core(piece(term, 2, core + 1))
    own = piece(half, n_y, y)
    for step in range(1, n_y):
        own = own + from_y(piece(half, n_y, y - step), step)
    part = 4
    for inner in (True, False):
        got = own
        for step in range(1, part):
            if inner:
                route = [(r, r // part * part + (r % part + step) % part) for r in range(n_rows)]
            else:
                route = ring(n_rows, step * part)
            got = got + lax.ppermute(own, "rows", route)
        own = got
    blocks = jnp.zeros((n_y,) + own.shape, f32)
    blocks = lax.dynamic_update_index_in_dim(blocks, own, y, 0)
    for step in range(1, n_y):
        blocks = lax.dynamic_update_index_in_dim(blocks, from_y(own, step), jnp.mod(y + step, n_y), 0)
    half = blocks.reshape(half.shape)
    other = from_core(half)
    return jnp.where(core == 0, jnp.concatenate([half, other]), jnp.concatenate([other, half]))


def local(features, weight, tile_values, tile_cols, tile_live, cotangent):
    n_rows = lax.axis_size("rows")
    n_rep = lax.axis_size("rep")
    rep = lax.axis_index("rep")
    node_dev, width = features.shape
    tile = tile_values.shape[2]
    own = node_dev // tile
    group_tiles = own * n_rep
    pieces = pieces_of(own)
    order = [key for _, keys in pieces for key in keys]
    table = np.zeros((3, n_rep // 2, own), np.int32)
    for at, key in enumerate(order):
        table[key] = at
    place = jnp.mod(tile_cols // group_tiles - lax.axis_index("rows") + 1, n_rows)
    inner = tile_cols % group_tiles
    owner = inner // own
    dy = jnp.mod(owner // 2 - rep // 2, n_rep // 2)
    dcore = jnp.mod(owner + rep, 2)
    key = (place * (n_rep // 2) + dy) * own + inner % own
    hit = key[:, :, None] == jnp.arange(table.size, dtype=jnp.int32)
    at = jnp.sum(jnp.where(hit, jnp.asarray(table.reshape(-1)), 0), axis=2)
    idx = dcore * table.size + at
    cnt = jnp.sum(tile_live, axis=1)

    got = gather(features, tile, own)
    mine = [got[name] for name, _ in pieces]
    parts = mine + [from_core(x) for x in mine]
    size = {name: len(keys) for name, keys in pieces}
    groups = [sum(size[name] for name in names) for names in GROUPS]
    output, term, *grads = layer(
        idx, cnt, tile_values, parts, weight, cotangent, list(size.values()), groups
    )
    total = scatter(grads[: len(groups)], grads[len(groups) :], own)
    weight_grad = weight_sum(term, n_rows, n_rep)
    feature_grad = jnp.swapaxes(total, 1, 2).reshape(node_dev, width).astype(bf16)
    return (output, feature_grad, weight_grad)


def solution(mesh):
    placed = (
        P(("rows", "rep"), None),
        P(),
        P(("rows", "rep"), None, None, None),
        P(("rows", "rep"), None),
        P(("rows", "rep"), None),
        P(("rows", "rep"), None),
    )
    return jax.shard_map(
        local,
        mesh=mesh,
        in_specs=placed,
        out_specs=(P(("rows", "rep"), None), P(("rows", "rep"), None), P()),
        check_vma=False,
    )
```

```python
import functools
import math

import jax
import jax.numpy as jnp
import numpy as np
from jax import lax
from jax.experimental import pallas as pl
from jax.experimental.pallas import tpu as pltpu
from jax.sharding import PartitionSpec as P

bf16, f32 = jnp.bfloat16, jnp.float32

FWD_SLOTS = 12
BWD_SLOTS = 8
STAGES = 4


def layout(own, core):
    half = own // 2

    def shards(*keys):
        return [(p, dy, i) for p, dy in keys for i in range(own)]

    if core == 0:
        last = shards((1, 2), (0, 2), (2, 2))
        middle = shards((1, 1), (0, 1), (2, 1), (1, 3), (0, 3), (2, 3))
        first = [None] * own + shards((1, 0), (0, 0), (2, 0))
    else:
        last = shards((0, 2)) + [None] * half + shards((2, 2)) + [None] * half
        middle = shards((0, 0), (0, 1), (0, 3), (2, 0), (2, 1), (2, 3))
        first = shards((1, 2), (1, 0), (1, 1), (1, 3))
    return last, middle, first


def kernel(n_in, n_out, chunk, idx, cnt, a_ref, *refs):
    parts = refs[:n_in]
    w_ref, cot_ref, out_ref, wg_ref = refs[n_in : n_in + 4]
    outs = refs[n_in + 4 : n_in + 4 + n_out]
    win, acc, stage, in_sem, out_sem = refs[n_in + 4 + n_out :]
    t = pl.program_id(0)
    tile = a_ref.shape[2]

    @pl.when(t == 0)
    def _():
        copies, at = [], 0
        for k, part in enumerate(parts):
            rows = part.shape[0]
            copies.append(pltpu.make_async_copy(part, win.at[pl.ds(at, rows)], in_sem.at[k]))
            copies[-1].start()
            at += rows
        wg_ref[...] = jnp.zeros_like(wg_ref)

        def zero(i, _):
            acc[pl.ds(i * 4, 4)] = jnp.zeros((4,) + acc.shape[1:], f32)
            return 0

        lax.fori_loop(0, acc.shape[0] // 4, zero, 0)
        for copy in copies:
            copy.wait()

    n = cnt[t]

    def lanes(k0, count):
        got = []
        for j in range(count):
            a = a_ref[0, k0 + j]
            got.append(jnp.where(k0 + j < n, a, jnp.zeros_like(a)))
        return jnp.concatenate(got, axis=1)

    def forward(i, af):
        k0 = i * FWD_SLOTS
        rows = [
            win[pl.ds(pl.multiple_of(idx[t, k0 + j] * tile, tile), tile), :]
            for j in range(FWD_SLOTS)
        ]
        return af + jnp.dot(
            lanes(k0, FWD_SLOTS), jnp.concatenate(rows, axis=0), preferred_element_type=f32
        )

    width = w_ref.shape[0]
    trips = (n + FWD_SLOTS - 1) // FWD_SLOTS
    af = lax.fori_loop(0, trips, forward, jnp.zeros((tile, width), f32)).astype(bf16)
    pre = jnp.dot(af, w_ref[...], preferred_element_type=f32)
    sig = jax.nn.sigmoid(pre)
    out_ref[...] = (pre * sig).astype(bf16)
    g = (cot_ref[...].astype(f32) * sig * (1.0 + pre * (1.0 - sig))).astype(bf16)
    wg_ref[...] += lax.dot_general(af, g, (((0,), (0,)), ((), ())), preferred_element_type=f32)
    gwt = lax.dot_general(
        w_ref[...], g, (((1,), (1,)), ((), ())), preferred_element_type=f32
    ).astype(bf16)

    def backward(i, _):
        k0 = i * BWD_SLOTS
        r = jnp.dot(gwt, lanes(k0, BWD_SLOTS), preferred_element_type=f32)
        for j in range(BWD_SLOTS):
            acc[idx[t, k0 + j]] += r[:, j * tile : (j + 1) * tile]
        return 0

    lax.fori_loop(0, (n + BWD_SLOTS - 1) // BWD_SLOTS, backward, 0)

    @pl.when(t == pl.num_programs(0) - 1)
    def _():
        def copy(slot, out, at):
            return pltpu.make_async_copy(stage.at[slot], out.at[pl.ds(at, chunk)], out_sem.at[slot])

        done = 0
        for out in outs:
            steps = out.shape[0] // chunk

            def emit(i, _, out=out, done=done):
                number = done + i
                slot = lax.rem(number, STAGES)

                @pl.when(number >= STAGES)
                def _():
                    copy(slot, out, 0).wait()

                stage[slot] = acc[pl.ds(number * chunk, chunk)].astype(bf16)
                copy(slot, out, i * chunk).start()
                return 0

            lax.fori_loop(0, steps, emit, 0)
            done += steps
        for slot in range(STAGES):
            copy(slot, outs[0], 0).wait()


def layer(idx, cnt, tile_values, parts, weight, cotangent, groups):
    nt, slots, tile, _ = tile_values.shape
    width = weight.shape[0]
    n_win = 2 * sum(groups)
    chunk = math.gcd(*groups)
    anywhere = pl.BlockSpec(memory_space=pl.ANY)
    return pl.pallas_call(
        functools.partial(kernel, len(parts), 2 * len(groups), chunk),
        grid_spec=pltpu.PrefetchScalarGridSpec(
            num_scalar_prefetch=2,
            grid=(nt,),
            in_specs=[pl.BlockSpec((1, slots, tile, tile), lambda t, *_: (t, 0, 0, 0))]
            + [anywhere] * len(parts)
            + [
                pl.BlockSpec((width, width), lambda t, *_: (0, 0)),
                pl.BlockSpec((tile, width), lambda t, *_: (t, 0)),
            ],
            out_specs=[
                pl.BlockSpec((tile, width), lambda t, *_: (t, 0)),
                pl.BlockSpec((width, width), lambda t, *_: (0, 0)),
            ]
            + [anywhere] * (2 * len(groups)),
            scratch_shapes=[
                pltpu.VMEM((n_win * tile, width), bf16),
                pltpu.VMEM((n_win, width, tile), f32),
                pltpu.VMEM((STAGES, chunk, width, tile), bf16),
                pltpu.SemaphoreType.DMA((len(parts),)),
                pltpu.SemaphoreType.DMA((STAGES,)),
            ],
        ),
        out_shape=[
            jax.ShapeDtypeStruct((nt * tile, width), bf16),
            jax.ShapeDtypeStruct((width, width), f32),
        ]
        + [jax.ShapeDtypeStruct((g, width, tile), bf16) for _ in range(2) for g in groups],
        compiler_params=pltpu.CompilerParams(vmem_limit_bytes=60 * 2**20),
    )(idx, cnt, tile_values, *parts, weight, cotangent)


def near(group, rep, axis, step, n_rows, n_rep):
    if axis == "z":
        return (group + step) % n_rows * n_rep + rep
    return group * n_rep + (rep + 2 * step) % n_rep


def moved(x, moves, back=False):
    n_rows, n_rep = lax.axis_size("rows"), lax.axis_size("rep")
    pairs = []
    for group in range(n_rows):
        for rep in range(n_rep):
            if moves[rep % 2]:
                source = near(group, rep, *moves[rep % 2], n_rows, n_rep)
                pairs.append((source, group * n_rep + rep))
    if back:
        pairs = [(target, source) for source, target in pairs]
    return lax.ppermute(x, ("rows", "rep"), pairs)


FIRST_UP, FIRST_DOWN = (("z", -1), ("y", 1)), (("z", 1), ("y", -1))
HALF_UP, HALF_DOWN = (None, ("y", 1)), (None, ("y", -1))
NEXT_UP, NEXT_DOWN = (("y", 1), ("z", -1)), (("y", -1), ("z", 1))


def from_core(x):
    return lax.ppermute(x, "rep", [(i, i ^ 1) for i in range(lax.axis_size("rep"))])


def gather(features, core):
    rows = features.shape[0]
    half = rows // 2
    up, down = moved(features, FIRST_UP), moved(features, FIRST_DOWN)
    near3 = jnp.concatenate([features, up, down])
    far = jnp.concatenate([moved(up[:half], HALF_UP), moved(down[half:], HALF_DOWN)])
    up, down = moved(near3, NEXT_UP), moved(near3, NEXT_DOWN)
    crossing = jnp.concatenate([far, far[:half]])
    last_up = moved(jnp.where(core == 0, up[: 3 * half], crossing), NEXT_UP)
    last_down = moved(jnp.where(core == 0, down[3 * half :], crossing), NEXT_DOWN)
    mine = [last_up, last_down, up, down, far, near3]
    return mine + [from_core(x) for x in mine]


def scatter(mine, other, own, core):
    last, middle, first = (
        m.astype(f32) + from_core(o).astype(f32) for m, o in zip(mine, other)
    )
    half = own // 2
    cut = 3 * half
    last = last.astype(bf16)
    last_up = moved(last[:cut], NEXT_UP, back=True).astype(f32)
    last_down = moved(last[cut:], NEXT_DOWN, back=True).astype(f32)
    up, down = middle[: 2 * cut], middle[2 * cut :]
    along = (core == 0).astype(f32)
    up = jnp.concatenate([up[:cut] + along * last_up, up[cut:]]).astype(bf16)
    down = jnp.concatenate([down[:cut], down[cut:] + along * last_down]).astype(bf16)
    far = (first[:own] + (1.0 - along) * (last_up[:own] + last_down[:own])).astype(bf16)
    half_up = moved(far[:half], HALF_UP, back=True).astype(f32)
    half_down = moved(far[half:], HALF_DOWN, back=True).astype(f32)
    near3 = (
        first[own:]
        + moved(up, NEXT_UP, back=True).astype(f32)
        + moved(down, NEXT_DOWN, back=True).astype(f32)
    )
    home, up, down = near3[:own], near3[own : 2 * own], near3[2 * own :]
    up = jnp.concatenate([up[:half] + half_up, up[half:]]).astype(bf16)
    down = jnp.concatenate([down[:half], down[half:] + half_down]).astype(bf16)
    return (
        home
        + moved(up, FIRST_UP, back=True).astype(f32)
        + moved(down, FIRST_DOWN, back=True).astype(f32)
    )


def weight_sum(term, core):
    height = term.shape[0] // 2
    low, high = term[:height], term[height:]
    x = jnp.where(core == 0, low, high) + from_core(jnp.where(core == 0, high, low))
    for axis, first in (("rep", 2), ("rows", 1)):
        bit = first
        while bit < lax.axis_size(axis):
            pairs = [(i, i ^ bit) for i in range(lax.axis_size(axis))]
            x = x + lax.ppermute(x, axis, pairs)
            bit *= 2
    other = from_core(x)
    return jnp.where(core == 0, jnp.concatenate([x, other]), jnp.concatenate([other, x]))


def local(features, weight, tile_values, tile_cols, tile_live, cotangent):
    n_rows, n_rep = lax.axis_size("rows"), lax.axis_size("rep")
    rep = lax.axis_index("rep")
    node_dev, width = features.shape
    tile = tile_values.shape[2]
    own = node_dev // tile
    group_tiles = own * n_rep
    core = rep % 2
    plans = [layout(own, c) for c in range(2)]
    groups = [len(keys) for keys in plans[0]]
    table = np.zeros((2, 3, n_rep // 2, own), np.int32)
    for c, plan in enumerate(plans):
        for at, key in enumerate(sum(plan, [])):
            if key:
                table[(c, *key)] = at
    place = jnp.mod(tile_cols // group_tiles - lax.axis_index("rows") + 1, n_rows)
    inner = tile_cols % group_tiles
    owner = inner // own
    dy = jnp.mod(owner // 2 - rep // 2, n_rep // 2)
    key = (((owner % 2) * 3 + place) * (n_rep // 2) + dy) * own + inner % own
    hit = key[:, :, None] == jnp.arange(table.size, dtype=jnp.int32)
    at = jnp.sum(jnp.where(hit, jnp.asarray(table.reshape(-1)), 0), axis=2)
    idx = jnp.mod(owner + rep, 2) * sum(groups) + at
    cnt = jnp.sum(tile_live, axis=1)

    parts = gather(features, core)
    output, term, *grads = layer(idx, cnt, tile_values, parts, weight, cotangent, groups)
    total = scatter(grads[: len(groups)], grads[len(groups) :], own, core)
    weight_grad = weight_sum(term, core)
    feature_grad = jnp.swapaxes(total, 1, 2).reshape(node_dev, width).astype(bf16)
    return (output, feature_grad, weight_grad)


def solution(mesh):
    placed = (
        P(("rows", "rep"), None),
        P(),
        P(("rows", "rep"), None, None, None),
        P(("rows", "rep"), None),
        P(("rows", "rep"), None),
        P(("rows", "rep"), None),
    )
    return jax.shard_map(
        local,
        mesh=mesh,
        in_specs=placed,
        out_specs=(P(("rows", "rep"), None), P(("rows", "rep"), None), P()),
        check_vma=False,
    )
```

```python
import functools

import jax
import jax.numpy as jnp
import numpy as np
from jax import lax
from jax.experimental import pallas as pl
from jax.experimental.pallas import tpu as pltpu
from jax.sharding import PartitionSpec as P

bf16, f32 = jnp.bfloat16, jnp.float32

FWD_SLOTS = 12
BWD_SLOTS = 8
STAGES = 4


def layout(own, core):
    half = own // 2

    def shards(*keys):
        return [(p, dy, i) for p, dy in keys for i in range(own)]

    if core == 0:
        last = shards((1, 2), (0, 2), (2, 2))
        middle = shards((1, 1), (0, 1), (2, 1), (1, 3), (0, 3), (2, 3))
        first = [None] * own + shards((1, 0), (0, 0), (2, 0))
    else:
        last = shards((0, 2)) + [None] * half + shards((2, 2)) + [None] * half
        middle = shards((0, 0), (0, 1), (0, 3), (2, 0), (2, 1), (2, 3))
        first = shards((1, 2), (1, 0), (1, 1), (1, 3))
    return last, middle, first


def lanes(a_ref, order, t, k0, end, count):
    got = []
    for j in range(count):
        a = a_ref[0, order[t, k0 + j]]
        got.append(jnp.where(k0 + j < end, a, jnp.zeros_like(a)))
    return jnp.concatenate(got, axis=1)


def clear(acc):
    def zero(i, _):
        acc[pl.ds(i * 4, 4)] = jnp.zeros((4,) + acc.shape[1:], f32)
        return 0

    lax.fori_loop(0, acc.shape[0] // 4, zero, 0)


def spread(a_ref, acc, gwt, order, at, t, begin, end, base):
    tile = a_ref.shape[2]

    def body(i, _):
        k0 = begin + i * BWD_SLOTS
        r = jnp.dot(gwt, lanes(a_ref, order, t, k0, end, BWD_SLOTS), preferred_element_type=f32)
        for j in range(BWD_SLOTS):
            c = jnp.where(k0 + j < end, at[t, k0 + j] - base, 0)
            acc[c] += r[:, j * tile : (j + 1) * tile]
        return 0

    lax.fori_loop(0, (end - begin + BWD_SLOTS - 1) // BWD_SLOTS, body, 0)


def hand_out(acc, outs, stage, sem):
    chunk = stage.shape[1]

    def copy(slot, out, at):
        return pltpu.make_async_copy(stage.at[slot], out.at[pl.ds(at, chunk)], sem.at[slot])

    done = 0
    for out in outs:
        steps = out.shape[0] // chunk

        def emit(i, _, out=out, done=done):
            number = done + i
            slot = lax.rem(number, STAGES)

            @pl.when(number >= STAGES)
            def _():
                copy(slot, out, 0).wait()

            stage[slot] = acc[pl.ds(number * chunk, chunk)].astype(bf16)
            copy(slot, out, i * chunk).start()
            return 0

        lax.fori_loop(0, steps, emit, 0)
        done += steps
    for slot in range(STAGES):
        copy(slot, outs[0], 0).wait()


def whole_kernel(n_in, order, at, ends, a_ref, *refs):
    parts = refs[:n_in]
    w_ref, cot_ref, out_ref, wg_ref, gwt_ref = refs[n_in : n_in + 5]
    outs = refs[n_in + 5 : n_in + 7]
    win, acc, stage, in_sem, out_sem = refs[n_in + 7 :]
    t = pl.program_id(0)
    tile, width = a_ref.shape[2], w_ref.shape[0]

    @pl.when(t == 0)
    def _():
        copies, row = [], 0
        for k, part in enumerate(parts):
            rows = part.shape[0]
            copies.append(pltpu.make_async_copy(part, win.at[pl.ds(row, rows)], in_sem.at[k]))
            copies[-1].start()
            row += rows
        wg_ref[...] = jnp.zeros_like(wg_ref)
        clear(acc)
        for copy in copies:
            copy.wait()

    n = ends[t, 2]

    def forward(i, af):
        k0 = i * FWD_SLOTS
        rows = [
            win[pl.ds(pl.multiple_of(at[t, k0 + j] * tile, tile), tile), :]
            for j in range(FWD_SLOTS)
        ]
        a = lanes(a_ref, order, t, k0, n, FWD_SLOTS)
        return af + jnp.dot(a, jnp.concatenate(rows, axis=0), preferred_element_type=f32)

    trips = (n + FWD_SLOTS - 1) // FWD_SLOTS
    af = lax.fori_loop(0, trips, forward, jnp.zeros((tile, width), f32)).astype(bf16)
    pre = jnp.dot(af, w_ref[...], preferred_element_type=f32)
    sig = jax.nn.sigmoid(pre)
    out_ref[...] = (pre * sig).astype(bf16)
    g = (cot_ref[...].astype(f32) * sig * (1.0 + pre * (1.0 - sig))).astype(bf16)
    wg_ref[...] += lax.dot_general(af, g, (((0,), (0,)), ((), ())), preferred_element_type=f32)
    gwt = lax.dot_general(
        w_ref[...], g, (((1,), (1,)), ((), ())), preferred_element_type=f32
    ).astype(bf16)
    gwt_ref[0] = gwt
    spread(a_ref, acc, gwt, order, at, t, 0, ends[t, 0], 0)

    @pl.when(t == pl.num_programs(0) - 1)
    def _():
        hand_out(acc, outs, stage, out_sem)


def back_kernel(group, base, order, at, ends, a_ref, gwt_ref, *refs):
    mine, other, acc, stage, sem = refs[-5:]
    t = pl.program_id(0)

    @pl.when(t == 0)
    def _():
        clear(acc)

    spread(a_ref, acc, gwt_ref[0], order, at, t, ends[t, group - 1], ends[t, group], base)

    @pl.when(t == pl.num_programs(0) - 1)
    def _():
        hand_out(acc, (mine, other), stage, sem)


ANYWHERE = pl.BlockSpec(memory_space=pl.ANY)
CHUNK = 8


def back_scratch(size, width, tile):
    return [
        pltpu.VMEM((2 * size, width, tile), f32),
        pltpu.VMEM((STAGES, CHUNK, width, tile), bf16),
    ]


def values_block(tile_values):
    return pl.BlockSpec((1,) + tile_values.shape[1:], lambda t, *_: (t, 0, 0, 0))


def handed(size, width, tile):
    return [jax.ShapeDtypeStruct((size, width, tile), bf16)] * 2


def cost(tile_values, width, products, passes):
    return pl.CostEstimate(
        flops=products * tile_values.size * width,
        bytes_accessed=passes * 2 * tile_values.size,
        transcendentals=0,
    )


def front(lists, tile_values, parts, weight, cotangent, groups):
    nt, _, tile, _ = tile_values.shape
    width = weight.shape[0]
    output, term, gwt, mine, other = pl.pallas_call(
        functools.partial(whole_kernel, len(parts)),
        grid_spec=pltpu.PrefetchScalarGridSpec(
            num_scalar_prefetch=3,
            grid=(nt,),
            in_specs=[values_block(tile_values)]
            + [ANYWHERE] * len(parts)
            + [
                pl.BlockSpec((width, width), lambda t, *_: (0, 0)),
                pl.BlockSpec((tile, width), lambda t, *_: (t, 0)),
            ],
            out_specs=[
                pl.BlockSpec((tile, width), lambda t, *_: (t, 0)),
                pl.BlockSpec((width, width), lambda t, *_: (0, 0)),
                pl.BlockSpec((1, width, tile), lambda t, *_: (t, 0, 0)),
                ANYWHERE,
                ANYWHERE,
            ],
            scratch_shapes=[pltpu.VMEM((2 * sum(groups) * tile, width), bf16)]
            + back_scratch(groups[0], width, tile)
            + [pltpu.SemaphoreType.DMA((len(parts),)), pltpu.SemaphoreType.DMA((STAGES,))],
        ),
        out_shape=[
            jax.ShapeDtypeStruct((nt * tile, width), bf16),
            jax.ShapeDtypeStruct((width, width), f32),
            jax.ShapeDtypeStruct((nt, width, tile), bf16),
        ]
        + handed(groups[0], width, tile),
        compiler_params=pltpu.CompilerParams(vmem_limit_bytes=60 * 2**20),
        cost_estimate=cost(tile_values, width, 3, 3),
    )(*lists, tile_values, *parts, weight, cotangent)
    return output, term, gwt, mine, other


def rest(lists, tile_values, gwt, group, groups, earlier=()):
    nt, _, tile, _ = tile_values.shape
    width = gwt.shape[1]
    return pl.pallas_call(
        functools.partial(back_kernel, group, 2 * sum(groups[:group])),
        grid_spec=pltpu.PrefetchScalarGridSpec(
            num_scalar_prefetch=3,
            grid=(nt,),
            in_specs=[
                values_block(tile_values),
                pl.BlockSpec((1, width, tile), lambda t, *_: (t, 0, 0)),
            ]
            + [ANYWHERE] * len(earlier),
            out_specs=[ANYWHERE, ANYWHERE],
            scratch_shapes=back_scratch(groups[group], width, tile)
            + [pltpu.SemaphoreType.DMA((STAGES,))],
        ),
        out_shape=handed(groups[group], width, tile),
        compiler_params=pltpu.CompilerParams(vmem_limit_bytes=60 * 2**20),
        cost_estimate=cost(tile_values, width, 1, 2),
    )(*lists, tile_values, gwt, *earlier)


def tied(x, *earlier):
    return pl.pallas_call(
        lambda *refs: None,
        in_specs=[ANYWHERE] * (1 + len(earlier)),
        out_specs=ANYWHERE,
        out_shape=jax.ShapeDtypeStruct(x.shape, x.dtype),
        input_output_aliases={0: 0},
    )(x, *earlier)


def near(group, rep, axis, step, n_rows, n_rep):
    if axis == "z":
        return (group + step) % n_rows * n_rep + rep
    return group * n_rep + (rep + 2 * step) % n_rep


def moved(x, moves, back=False):
    n_rows, n_rep = lax.axis_size("rows"), lax.axis_size("rep")
    pairs = []
    for group in range(n_rows):
        for rep in range(n_rep):
            if moves[rep % 2]:
                source = near(group, rep, *moves[rep % 2], n_rows, n_rep)
                pairs.append((source, group * n_rep + rep))
    if back:
        pairs = [(target, source) for source, target in pairs]
    return lax.ppermute(x, ("rows", "rep"), pairs)


FIRST_UP, FIRST_DOWN = (("z", -1), ("y", 1)), (("z", 1), ("y", -1))
HALF_UP, HALF_DOWN = (None, ("y", 1)), (None, ("y", -1))
NEXT_UP, NEXT_DOWN = (("y", 1), ("z", -1)), (("y", -1), ("z", 1))


def from_core(x):
    return lax.ppermute(x, "rep", [(i, i ^ 1) for i in range(lax.axis_size("rep"))])


def gather(features, core):
    rows = features.shape[0]
    half = rows // 2
    up, down = moved(features, FIRST_UP), moved(features, FIRST_DOWN)
    near3 = jnp.concatenate([features, up, down])
    far = jnp.concatenate([moved(up[:half], HALF_UP), moved(down[half:], HALF_DOWN)])
    up, down = moved(near3, NEXT_UP), moved(near3, NEXT_DOWN)
    crossing = jnp.concatenate([far, far[:half]])
    last_up = moved(jnp.where(core == 0, up[: 3 * half], crossing), NEXT_UP)
    last_down = moved(jnp.where(core == 0, down[3 * half :], crossing), NEXT_DOWN)
    mine = ((last_up, last_down), (up, down), (far, near3))
    return [x for pair in mine for part in (pair, [from_core(x) for x in pair]) for x in part]


def joined(mine, other):
    return mine.astype(f32) + from_core(other).astype(f32)


def scatter(last, middle, first, own, core, steps):
    half = own // 2
    cut = 3 * half
    last_up, last_down = (x.astype(f32) for x in last)
    up, down = middle[: 2 * cut], middle[2 * cut :]
    along = (core == 0).astype(f32)
    up = jnp.concatenate([up[:cut] + along * last_up, up[cut:]]).astype(bf16)
    down = jnp.concatenate([down[:cut], down[cut:] + along * last_down]).astype(bf16)
    next_up, next_down = moved(up, NEXT_UP, back=True), moved(down, NEXT_DOWN, back=True)
    steps.go(2)
    far = (first[:own] + (1.0 - along) * (last_up[:own] + last_down[:own])).astype(bf16)
    half_up = moved(far[:half], HALF_UP, back=True)
    half_down = moved(far[half:], HALF_DOWN, back=True)
    steps.tie(half_up, half_down)
    steps.go(2)
    near3 = first[own:] + next_up.astype(f32) + next_down.astype(f32)
    home, up, down = near3[:own], near3[own : 2 * own], near3[2 * own :]
    up = jnp.concatenate([up[:half] + half_up.astype(f32), up[half:]]).astype(bf16)
    down = jnp.concatenate([down[:half], down[half:] + half_down.astype(f32)]).astype(bf16)
    up = tied(up, steps.x)
    return (
        home
        + moved(up, FIRST_UP, back=True).astype(f32)
        + moved(down, FIRST_DOWN, back=True).astype(f32)
    )


class Steps:
    def __init__(self, term, core):
        height = term.shape[0] // 2
        low, high = term[:height], term[height:]
        self.got = from_core(jnp.where(core == 0, high, low))
        self.x = jnp.where(core == 0, low, high) + self.got
        self.left = [
            (axis, bit)
            for axis, first in (("rep", 2), ("rows", 1))
            for bit in (1 << k for k in range(10))
            if first <= bit < lax.axis_size(axis)
        ]

    def go(self, count):
        for axis, bit in self.left[:count]:
            pairs = [(i, i ^ bit) for i in range(lax.axis_size(axis))]
            self.got = lax.ppermute(self.x, axis, pairs)
            self.x = self.x + self.got
        self.left = self.left[count:]

    def tie(self, *earlier):
        self.x = tied(self.x, *earlier)

    def whole(self, core):
        self.go(len(self.left))
        other = from_core(self.x)
        halves = [self.x, other], [other, self.x]
        return jnp.where(core == 0, *(jnp.concatenate(h) for h in halves))


def by_group(at, live, starts):
    slots = at.shape[1]
    group = sum((at >= start).astype(jnp.int32) for start in starts[1:])
    group = jnp.where(live > 0, group, len(starts))
    ends = jnp.stack([jnp.sum(group <= g, axis=1) for g in range(len(starts))], axis=1)
    s = jnp.arange(slots, dtype=jnp.int32)
    a, b = group[:, :, None], group[:, None, :]
    before = (b < a) | ((b == a) & (s[None, :] < s[:, None]))
    rank = jnp.sum(before, axis=2)
    k = jnp.arange(slots + 16, dtype=jnp.int32)
    hit = (rank[:, None, :] == k[:, None]) & (live > 0)[:, None, :]
    order = jnp.sum(jnp.where(hit, s, 0), axis=2)
    place = jnp.sum(jnp.where(hit, at[:, None, :], 0), axis=2)
    return order.astype(jnp.int32), place.astype(jnp.int32), ends.astype(jnp.int32)


def local(features, weight, tile_values, tile_cols, tile_live, cotangent):
    n_rows, n_rep = lax.axis_size("rows"), lax.axis_size("rep")
    rep = lax.axis_index("rep")
    node_dev, width = features.shape
    tile = tile_values.shape[2]
    own = node_dev // tile
    group_tiles = own * n_rep
    core = rep % 2
    plans = [layout(own, c) for c in range(2)]
    groups = [len(keys) for keys in plans[0]]
    starts = [2 * sum(groups[:g]) for g in range(len(groups))]
    table = np.zeros((2, 3, n_rep // 2, own), np.int32)
    stride = np.zeros_like(table)
    for c, plan in enumerate(plans):
        for start, keys in zip(starts, plan):
            for at, key in enumerate(keys):
                if key:
                    table[(c, *key)] = start + at
                    stride[(c, *key)] = len(keys)
    place = jnp.mod(tile_cols // group_tiles - lax.axis_index("rows") + 1, n_rows)
    inner = tile_cols % group_tiles
    owner = inner // own
    dy = jnp.mod(owner // 2 - rep // 2, n_rep // 2)
    key = (((owner % 2) * 3 + place) * (n_rep // 2) + dy) * own + inner % own
    hit = key[:, :, None] == jnp.arange(table.size, dtype=jnp.int32)
    turn = jnp.mod(owner + rep, 2)[:, :, None]
    spot = jnp.asarray(table.reshape(-1)) + turn * jnp.asarray(stride.reshape(-1))
    at = jnp.sum(jnp.where(hit, spot, 0), axis=2)
    lists = by_group(at, tile_live, starts)

    parts = gather(features, core)
    output, term, gwt, mine, other = front(lists, tile_values, parts, weight, cotangent, groups)
    last = joined(mine, other).astype(bf16)
    steps = Steps(term, core)
    cut = groups[0] // 2
    sent = last[:cut], last[cut:]
    mine, other = rest(lists, tile_values, gwt, 1, groups)
    other = tied(other, steps.got)
    mine2, other2 = rest(lists, tile_values, gwt, 2, groups, (*sent, other))
    last = moved(sent[0], NEXT_UP, back=True), moved(sent[1], NEXT_DOWN, back=True)
    middle = joined(mine, other)
    steps.go(1)
    first = joined(mine2, tied(other2, *last, steps.got))
    total = scatter(last, middle, first, own, core, steps)
    weight_grad = steps.whole(core)
    feature_grad = jnp.swapaxes(total, 1, 2).reshape(node_dev, width).astype(bf16)
    return (output, feature_grad, weight_grad)


def solution(mesh):
    placed = (
        P(("rows", "rep"), None),
        P(),
        P(("rows", "rep"), None, None, None),
        P(("rows", "rep"), None),
        P(("rows", "rep"), None),
        P(("rows", "rep"), None),
    )
    return jax.shard_map(
        local,
        mesh=mesh,
        in_specs=placed,
        out_specs=(P(("rows", "rep"), None), P(("rows", "rep"), None), P()),
        check_vma=False,
    )
```

```python
import functools

import jax
import jax.numpy as jnp
import numpy as np
from jax import lax
from jax.experimental import pallas as pl
from jax.experimental.pallas import tpu as pltpu
from jax.sharding import PartitionSpec as P

bf16, f32 = jnp.bfloat16, jnp.float32

FWD_SLOTS = 24
BWD_SLOTS = 12
STAGES = 8
CHUNK = 8


def layout(own, core):
    half = own // 2

    def shards(*keys):
        return [(p, dy, i) for p, dy in keys for i in range(own)]

    if core == 0:
        last = shards((1, 2), (0, 2), (2, 2))
        middle = shards((1, 1), (0, 1), (2, 1), (1, 3), (0, 3), (2, 3))
        first = [None] * own + shards((1, 0), (0, 0), (2, 0))
    else:
        last = shards((0, 2)) + [None] * half + shards((2, 2)) + [None] * half
        middle = shards((0, 0), (0, 1), (0, 3), (2, 0), (2, 1), (2, 3))
        first = shards((1, 2), (1, 0), (1, 1), (1, 3))
    return last, middle, first


def kernel(n_in, n_out, idx, cnt, values, *refs):
    parts = refs[:n_in]
    w_ref, cot_ref, out_ref, wg_ref = refs[n_in : n_in + 4]
    outs = refs[n_in + 4 : n_in + 4 + n_out]
    a_ref, win, acc, stage, in_sem, a_sem, out_sem = refs[n_in + 4 + n_out :]
    n_tiles, _, tile, _ = a_ref.shape
    width = w_ref.shape[0]
    copies, row = [], 0
    for k, part in enumerate(parts):
        rows = part.shape[0]
        copies.append(pltpu.make_async_copy(part, win.at[pl.ds(row, rows)], in_sem.at[k]))
        row += rows
    blocks = [pltpu.make_async_copy(values.at[t], a_ref.at[t], a_sem.at[t]) for t in range(n_tiles)]
    for copy in copies + blocks:
        copy.start()
    wg_ref[...] = jnp.zeros_like(wg_ref)

    def zero(i, _):
        acc[pl.ds(i * 8, 8)] = jnp.zeros((8,) + acc.shape[1:], f32)
        return 0

    lax.fori_loop(0, acc.shape[0] // 8, zero, 0)
    for copy in copies:
        copy.wait()

    def row_tile(t, _):
        pltpu.make_async_copy(values.at[t], a_ref.at[t], a_sem.at[t]).wait()
        n = cnt[t]

        def lanes(k0, count):
            got = []
            for j in range(count):
                a = a_ref[t, k0 + j]
                got.append(jnp.where(k0 + j < n, a, jnp.zeros_like(a)))
            return jnp.concatenate(got, axis=1)

        def forward(i, af):
            k0 = i * FWD_SLOTS
            rows = [
                win[pl.ds(pl.multiple_of(idx[t, k0 + j] * tile, tile), tile), :]
                for j in range(FWD_SLOTS)
            ]
            return af + jnp.dot(
                lanes(k0, FWD_SLOTS), jnp.concatenate(rows, axis=0), preferred_element_type=f32
            )

        at = pl.ds(pl.multiple_of(t * tile, tile), tile)
        trips = (n + FWD_SLOTS - 1) // FWD_SLOTS
        af = lax.fori_loop(0, trips, forward, jnp.zeros((tile, width), f32)).astype(bf16)
        pre = jnp.dot(af, w_ref[...], preferred_element_type=f32)
        sig = jax.nn.sigmoid(pre)
        out_ref[at, :] = (pre * sig).astype(bf16)
        g = (cot_ref[at, :].astype(f32) * sig * (1.0 + pre * (1.0 - sig))).astype(bf16)
        wg_ref[...] += lax.dot_general(
            af, g, (((0,), (0,)), ((), ())), preferred_element_type=f32
        )
        gwt = lax.dot_general(
            w_ref[...], g, (((1,), (1,)), ((), ())), preferred_element_type=f32
        ).astype(bf16)

        def backward(i, _):
            k0 = i * BWD_SLOTS
            r = jnp.dot(gwt, lanes(k0, BWD_SLOTS), preferred_element_type=f32)
            for j in range(BWD_SLOTS):
                acc[idx[t, k0 + j]] += r[:, j * tile : (j + 1) * tile]
            return 0

        lax.fori_loop(0, (n + BWD_SLOTS - 1) // BWD_SLOTS, backward, 0)
        return 0

    lax.fori_loop(0, n_tiles, row_tile, 0)
    stages, chunk = stage.shape[:2]

    def copy(slot, out, at):
        return pltpu.make_async_copy(stage.at[slot], out.at[pl.ds(at, chunk)], out_sem.at[slot])

    done = 0
    for out in outs:
        steps = out.shape[0] // chunk

        def emit(i, _, out=out, done=done):
            number = done + i
            slot = lax.rem(number, stages)

            @pl.when(number >= stages)
            def _():
                copy(slot, out, 0).wait()

            stage[slot] = acc[pl.ds(number * chunk, chunk)].astype(bf16)
            copy(slot, out, i * chunk).start()
            return 0

        lax.fori_loop(0, steps, emit, 0)
        done += steps
    for slot in range(stages):
        copy(slot, outs[0], 0).wait()


def layer(idx, cnt, tile_values, parts, weight, cotangent, groups):
    nt, _, tile, _ = tile_values.shape
    width = weight.shape[0]
    n_win = 2 * sum(groups)
    smem = pl.BlockSpec(memory_space=pltpu.SMEM)
    vmem = pl.BlockSpec(memory_space=pltpu.VMEM)
    anywhere = pl.BlockSpec(memory_space=pl.ANY)
    return pl.pallas_call(
        functools.partial(kernel, len(parts), 2 * len(groups)),
        in_specs=[smem, smem] + [anywhere] * (1 + len(parts)) + [vmem, vmem],
        out_specs=[vmem, vmem] + [anywhere] * (2 * len(groups)),
        scratch_shapes=[
            pltpu.VMEM(tile_values.shape, bf16),
            pltpu.VMEM((n_win * tile, width), bf16),
            pltpu.VMEM((n_win, width, tile), f32),
            pltpu.VMEM((STAGES, CHUNK, width, tile), bf16),
            pltpu.SemaphoreType.DMA((len(parts),)),
            pltpu.SemaphoreType.DMA((nt,)),
            pltpu.SemaphoreType.DMA((STAGES,)),
        ],
        out_shape=[
            jax.ShapeDtypeStruct((nt * tile, width), bf16),
            jax.ShapeDtypeStruct((width, width), f32),
        ]
        + [jax.ShapeDtypeStruct((g, width, tile), bf16) for _ in range(2) for g in groups],
        compiler_params=pltpu.CompilerParams(vmem_limit_bytes=60 * 2**20),
        cost_estimate=pl.CostEstimate(
            flops=4 * tile_values.size * width,
            bytes_accessed=6 * tile_values.size,
            transcendentals=0,
        ),
    )(idx, cnt, tile_values, *parts, weight, cotangent)


def tied(x, *earlier):
    return pl.pallas_call(
        lambda *refs: None,
        in_specs=[pl.BlockSpec(memory_space=pl.ANY)] * (1 + len(earlier)),
        out_specs=pl.BlockSpec(memory_space=pl.ANY),
        out_shape=jax.ShapeDtypeStruct(x.shape, x.dtype),
        input_output_aliases={0: 0},
    )(x, *earlier)


def never(*earlier):
    out = False
    for x in earlier:
        v = x[(0,) * x.ndim]
        out |= (v != v) & (v == v)
    return out


def near(group, rep, axis, step, n_rows, n_rep):
    if axis == "z":
        return (group + step) % n_rows * n_rep + rep
    return group * n_rep + (rep + 2 * step) % n_rep


def moved(x, moves, back=False):
    n_rows, n_rep = lax.axis_size("rows"), lax.axis_size("rep")
    pairs = []
    for group in range(n_rows):
        for rep in range(n_rep):
            if moves[rep % 2]:
                source = near(group, rep, *moves[rep % 2], n_rows, n_rep)
                pairs.append((source, group * n_rep + rep))
    if back:
        pairs = [(target, source) for source, target in pairs]
    return lax.ppermute(x, ("rows", "rep"), pairs)


FIRST_UP, FIRST_DOWN = (("z", -1), ("y", 1)), (("z", 1), ("y", -1))
HALF_UP, HALF_DOWN = (None, ("y", 1)), (None, ("y", -1))
NEXT_UP, NEXT_DOWN = (("y", 1), ("z", -1)), (("y", -1), ("z", 1))


def from_core(x):
    return lax.ppermute(x, "rep", [(i, i ^ 1) for i in range(lax.axis_size("rep"))])


def gather(features, core):
    rows = features.shape[0]
    half = rows // 2
    up, down = moved(features, FIRST_UP), moved(features, FIRST_DOWN)
    near3 = jnp.concatenate([features, up, down])
    far = jnp.concatenate([moved(up[:half], HALF_UP), moved(down[half:], HALF_DOWN)])
    up, down = moved(near3, NEXT_UP), moved(near3, NEXT_DOWN)
    crossing = jnp.concatenate([far, far[:half]])
    swapped = from_core(near3)
    first = (core == 0) | never(swapped)
    last_up = moved(jnp.where(first, up[: 3 * half], crossing), NEXT_UP)
    last_down = moved(jnp.where(first, down[3 * half :], crossing), NEXT_DOWN)
    mine = [last_up, last_down, up, down, far]
    return mine + [near3] + [from_core(x) for x in mine] + [swapped]


class Steps:
    def __init__(self, term, core):
        height = term.shape[0] // 2
        low, high = term[:height], term[height:]
        self.got = from_core(jnp.where(core == 0, high, low))
        self.x = jnp.where(core == 0, low, high) + self.got
        self.left = [
            (axis, bit)
            for axis, first in (("rep", 2), ("rows", 1))
            for bit in (1 << k for k in range(10))
            if first <= bit < lax.axis_size(axis)
        ]

    def go(self, count):
        for axis, bit in self.left[:count]:
            pairs = [(i, i ^ bit) for i in range(lax.axis_size(axis))]
            self.got = lax.ppermute(self.x, axis, pairs)
            self.x = self.x + self.got
        self.left = self.left[count:]

    def after(self, *earlier):
        self.x = jnp.where(never(*earlier), 0.0, self.x)

    def whole(self, core):
        self.go(len(self.left))
        other = from_core(self.x)
        halves = [self.x, other], [other, self.x]
        return jnp.where(core == 0, *(jnp.concatenate(h) for h in halves))


def scatter(mine, other, own, core, steps):
    half = own // 2
    cut = 3 * half
    last = (mine[0].astype(f32) + from_core(other[0]).astype(f32)).astype(bf16)
    begun = last[:1, :8]
    middle, first = (
        m.astype(f32) + from_core(tied(o, begun)).astype(f32)
        for m, o in zip(mine[1:], other[1:])
    )
    last_up = moved(last[:cut], NEXT_UP, back=True).astype(f32)
    last_down = moved(last[cut:], NEXT_DOWN, back=True).astype(f32)
    steps.go(2)
    up, down = middle[: 2 * cut], middle[2 * cut :]
    along = ((core == 0) | never(steps.x)).astype(f32)
    up = jnp.concatenate([up[:cut] + along * last_up, up[cut:]]).astype(bf16)
    down = jnp.concatenate([down[:cut], down[cut:] + along * last_down]).astype(bf16)
    across = (core != 0).astype(f32)
    far = (first[:own] + across * (last_up[:own] + last_down[:own])).astype(bf16)
    next_up, next_down = moved(up, NEXT_UP, back=True), moved(down, NEXT_DOWN, back=True)
    half_up = moved(far[:half], HALF_UP, back=True)
    half_down = moved(far[half:], HALF_DOWN, back=True)
    steps.go(1)
    steps.after(half_up, half_down)
    steps.go(2)
    near3 = first[own:] + next_up.astype(f32) + next_down.astype(f32)
    home, up, down = near3[:own], near3[own : 2 * own], near3[2 * own :]
    none = never(steps.x)
    up = jnp.concatenate([up[:half] + half_up.astype(f32), up[half:]])
    down = jnp.concatenate([down[:half], down[half:] + half_down.astype(f32)])
    up, down = (jnp.where(none, 0.0, x).astype(bf16) for x in (up, down))
    return (
        home
        + moved(up, FIRST_UP, back=True).astype(f32)
        + moved(down, FIRST_DOWN, back=True).astype(f32)
    )


def local(features, weight, tile_values, tile_cols, tile_live, cotangent):
    n_rows, n_rep = lax.axis_size("rows"), lax.axis_size("rep")
    rep = lax.axis_index("rep")
    node_dev, width = features.shape
    tile = tile_values.shape[2]
    own = node_dev // tile
    group_tiles = own * n_rep
    core = rep % 2
    plans = [layout(own, c) for c in range(2)]
    groups = [len(keys) for keys in plans[0]]
    table = np.zeros((2, 3, n_rep // 2, own), np.int32)
    for c, plan in enumerate(plans):
        for at, key in enumerate(sum(plan, [])):
            if key:
                table[(c, *key)] = at
    place = jnp.mod(tile_cols // group_tiles - lax.axis_index("rows") + 1, n_rows)
    inner = tile_cols % group_tiles
    owner = inner // own
    dy = jnp.mod(owner // 2 - rep // 2, n_rep // 2)
    key = (((owner % 2) * 3 + place) * (n_rep // 2) + dy) * own + inner % own
    hit = key[:, :, None] == jnp.arange(table.size, dtype=jnp.int32)
    at = jnp.sum(jnp.where(hit, jnp.asarray(table.reshape(-1)), 0), axis=2)
    idx = jnp.mod(owner + rep, 2) * sum(groups) + at
    cnt = jnp.sum(tile_live, axis=1)

    parts = gather(features, core)
    output, term, *grads = layer(idx, cnt, tile_values, parts, weight, cotangent, groups)
    steps = Steps(term, core)
    total = scatter(grads[: len(groups)], grads[len(groups) :], own, core, steps)
    weight_grad = steps.whole(core)
    feature_grad = jnp.swapaxes(total, 1, 2).reshape(node_dev, width).astype(bf16)
    return (output, feature_grad, weight_grad)


def solution(mesh):
    placed = (
        P(("rows", "rep"), None),
        P(),
        P(("rows", "rep"), None, None, None),
        P(("rows", "rep"), None),
        P(("rows", "rep"), None),
        P(("rows", "rep"), None),
    )
    return jax.shard_map(
        local,
        mesh=mesh,
        in_specs=placed,
        out_specs=(P(("rows", "rep"), None), P(("rows", "rep"), None), P()),
        check_vma=False,
    )
```

```python
import functools

import jax
import jax.numpy as jnp
import numpy as np
from jax import lax
from jax.experimental import pallas as pl
from jax.experimental.pallas import tpu as pltpu
from jax.sharding import PartitionSpec as P

bf16, f32 = jnp.bfloat16, jnp.float32

FWD_SLOTS = 24
BWD_SLOTS = 12
STAGES = 8
CHUNK = 8


def layout(own, core):
    half = own // 2

    def shards(*keys):
        return [(p, dy, i) for p, dy in keys for i in range(own)]

    if core == 0:
        last = shards((1, 2), (0, 2), (2, 2))
        middle = shards((1, 1), (0, 1), (2, 1), (1, 3), (0, 3), (2, 3))
        first = [None] * own + shards((1, 0), (0, 0), (2, 0))
    else:
        last = shards((0, 2)) + [None] * half + shards((2, 2)) + [None] * half
        middle = shards((0, 0), (0, 1), (0, 3), (2, 0), (2, 1), (2, 3))
        first = shards((1, 2), (1, 0), (1, 1), (1, 3))
    return last, middle, first


def kernel(n_in, n_out, idx, cnt, values, *refs):
    parts = refs[:n_in]
    w_ref, cot_ref, out_ref, wg_ref = refs[n_in : n_in + 4]
    outs = refs[n_in + 4 : n_in + 4 + n_out]
    a_ref, win, acc, stage, in_sem, a_sem, out_sem = refs[n_in + 4 + n_out :]
    n_tiles, _, tile, _ = a_ref.shape
    width = w_ref.shape[0]
    copies, row = [], 0
    for k, part in enumerate(parts):
        rows = part.shape[0]
        copies.append(pltpu.make_async_copy(part, win.at[pl.ds(row, rows)], in_sem.at[k]))
        row += rows
    blocks = [pltpu.make_async_copy(values.at[t], a_ref.at[t], a_sem.at[t]) for t in range(n_tiles)]
    for copy in copies + blocks:
        copy.start()
    wg_ref[...] = jnp.zeros_like(wg_ref)

    def zero(i, _):
        acc[pl.ds(i * 8, 8)] = jnp.zeros((8,) + acc.shape[1:], f32)
        return 0

    lax.fori_loop(0, acc.shape[0] // 8, zero, 0)
    for copy in copies:
        copy.wait()

    def row_tile(t, _):
        pltpu.make_async_copy(values.at[t], a_ref.at[t], a_sem.at[t]).wait()
        n = cnt[t]

        def lanes(k0, count):
            got = []
            for j in range(count):
                a = a_ref[t, k0 + j]
                got.append(jnp.where(k0 + j < n, a, jnp.zeros_like(a)))
            return jnp.concatenate(got, axis=1)

        def forward(i, af):
            k0 = i * FWD_SLOTS
            rows = [
                win[pl.ds(pl.multiple_of(idx[t, k0 + j] * tile, tile), tile), :]
                for j in range(FWD_SLOTS)
            ]
            return af + jnp.dot(
                lanes(k0, FWD_SLOTS), jnp.concatenate(rows, axis=0), preferred_element_type=f32
            )

        at = pl.ds(pl.multiple_of(t * tile, tile), tile)
        trips = (n + FWD_SLOTS - 1) // FWD_SLOTS
        af = lax.fori_loop(0, trips, forward, jnp.zeros((tile, width), f32)).astype(bf16)
        pre = jnp.dot(af, w_ref[...], preferred_element_type=f32)
        sig = jax.nn.sigmoid(pre)
        out_ref[at, :] = (pre * sig).astype(bf16)
        g = (cot_ref[at, :].astype(f32) * sig * (1.0 + pre * (1.0 - sig))).astype(bf16)
        wg_ref[...] += lax.dot_general(
            af, g, (((0,), (0,)), ((), ())), preferred_element_type=f32
        )
        gwt = lax.dot_general(
            w_ref[...], g, (((1,), (1,)), ((), ())), preferred_element_type=f32
        ).astype(bf16)

        def backward(i, _):
            k0 = i * BWD_SLOTS
            r = jnp.dot(gwt, lanes(k0, BWD_SLOTS), preferred_element_type=f32)
            for j in range(BWD_SLOTS):
                acc[idx[t, k0 + j]] += r[:, j * tile : (j + 1) * tile]
            return 0

        lax.fori_loop(0, (n + BWD_SLOTS - 1) // BWD_SLOTS, backward, 0)
        return 0

    lax.fori_loop(0, n_tiles, row_tile, 0)
    stages, chunk = stage.shape[:2]

    def copy(slot, out, at):
        return pltpu.make_async_copy(stage.at[slot], out.at[pl.ds(at, chunk)], out_sem.at[slot])

    done = 0
    for out in outs:
        steps = out.shape[0] // chunk

        def emit(i, _, out=out, done=done):
            number = done + i
            slot = lax.rem(number, stages)

            @pl.when(number >= stages)
            def _():
                copy(slot, out, 0).wait()

            stage[slot] = acc[pl.ds(number * chunk, chunk)].astype(bf16)
            copy(slot, out, i * chunk).start()
            return 0

        lax.fori_loop(0, steps, emit, 0)
        done += steps
    for slot in range(stages):
        copy(slot, outs[0], 0).wait()


def layer(idx, cnt, tile_values, parts, weight, cotangent, groups):
    nt, _, tile, _ = tile_values.shape
    width = weight.shape[0]
    n_win = 2 * sum(groups)
    smem = pl.BlockSpec(memory_space=pltpu.SMEM)
    vmem = pl.BlockSpec(memory_space=pltpu.VMEM)
    anywhere = pl.BlockSpec(memory_space=pl.ANY)
    return pl.pallas_call(
        functools.partial(kernel, len(parts), 2 * len(groups)),
        in_specs=[smem, smem] + [anywhere] * (1 + len(parts)) + [vmem, vmem],
        out_specs=[vmem, vmem] + [anywhere] * (2 * len(groups)),
        scratch_shapes=[
            pltpu.VMEM(tile_values.shape, bf16),
            pltpu.VMEM((n_win * tile, width), bf16),
            pltpu.VMEM((n_win, width, tile), f32),
            pltpu.VMEM((STAGES, CHUNK, width, tile), bf16),
            pltpu.SemaphoreType.DMA((len(parts),)),
            pltpu.SemaphoreType.DMA((nt,)),
            pltpu.SemaphoreType.DMA((STAGES,)),
        ],
        out_shape=[
            jax.ShapeDtypeStruct((nt * tile, width), bf16),
            jax.ShapeDtypeStruct((width, width), f32),
        ]
        + [jax.ShapeDtypeStruct((g, width, tile), bf16) for _ in range(2) for g in groups],
        compiler_params=pltpu.CompilerParams(vmem_limit_bytes=60 * 2**20),
        cost_estimate=pl.CostEstimate(
            flops=4 * tile_values.size * width,
            bytes_accessed=6 * tile_values.size,
            transcendentals=0,
        ),
    )(idx, cnt, tile_values, *parts, weight, cotangent)


def tied(x, *earlier):
    return pl.pallas_call(
        lambda *refs: None,
        in_specs=[pl.BlockSpec(memory_space=pl.ANY)] * (1 + len(earlier)),
        out_specs=pl.BlockSpec(memory_space=pl.ANY),
        out_shape=jax.ShapeDtypeStruct(x.shape, x.dtype),
        input_output_aliases={0: 0},
    )(x, *earlier)


def never(*earlier):
    out = False
    for x in earlier:
        v = x[(0,) * x.ndim]
        out |= (v != v) & (v == v)
    return out


def near(group, rep, axis, step, n_rows, n_rep):
    if axis == "z":
        return (group + step) % n_rows * n_rep + rep
    return group * n_rep + (rep + 2 * step) % n_rep


def moved(x, moves, back=False):
    n_rows, n_rep = lax.axis_size("rows"), lax.axis_size("rep")
    pairs = []
    for group in range(n_rows):
        for rep in range(n_rep):
            if moves[rep % 2]:
                source = near(group, rep, *moves[rep % 2], n_rows, n_rep)
                pairs.append((source, group * n_rep + rep))
    if back:
        pairs = [(target, source) for source, target in pairs]
    return lax.ppermute(x, ("rows", "rep"), pairs)


FIRST_UP, FIRST_DOWN = (("z", -1), ("y", 1)), (("z", 1), ("y", -1))
HALF_UP, HALF_DOWN = (None, ("y", 1)), (None, ("y", -1))
NEXT_UP, NEXT_DOWN = (("y", 1), ("z", -1)), (("y", -1), ("z", 1))


def from_core(x):
    return lax.ppermute(x, "rep", [(i, i ^ 1) for i in range(lax.axis_size("rep"))])


def gather(features, core):
    rows = features.shape[0]
    half = rows // 2
    up, down = moved(features, FIRST_UP), moved(features, FIRST_DOWN)
    near3 = jnp.concatenate([features, up, down])
    far = jnp.concatenate([moved(up[:half], HALF_UP), moved(down[half:], HALF_DOWN)])
    up, down = moved(near3, NEXT_UP), moved(near3, NEXT_DOWN)
    crossing = jnp.concatenate([far, far[:half]])
    swapped = from_core(near3)
    swapped_far = from_core(far)
    first = (core == 0) | never(swapped, swapped_far)
    last_up = moved(jnp.where(first, up[: 3 * half], crossing), NEXT_UP)
    last_down = moved(jnp.where(first, down[3 * half :], crossing), NEXT_DOWN)
    mine = [last_up, last_down, up, down]
    return mine + [far, near3] + [from_core(x) for x in mine] + [swapped_far, swapped]


def others(x, axis, group, stride):
    count = lax.axis_size(axis)
    got = []
    for step in range(1, group):
        pairs = []
        for i in range(count):
            digit = i // stride % group
            source = i + ((digit + step) % group - digit) * stride
            pairs.append((source, i))
        got.append((step, pairs))
    return [lax.ppermute(x(step), axis, pairs) for step, pairs in got]


class Steps:
    def __init__(self, term, core, y):
        height = term.shape[0] // 2
        low, high = term[:height], term[height:]
        half = jnp.where(core == 0, low, high) + from_core(jnp.where(core == 0, high, low))
        self.core, self.y, self.n_y = core, y, lax.axis_size("rep") // 2
        self.x = half.reshape(self.n_y, height // self.n_y, term.shape[1])

    def piece(self, at):
        return lax.dynamic_index_in_dim(self.x, jnp.mod(at, self.n_y), 0, keepdims=False)

    def scatter(self):
        got = others(lambda step: self.piece(self.y - step), "rep", self.n_y, 2)
        self.x = sum(got, self.piece(self.y))

    def sum_rows(self, stride):
        self.x = sum(others(lambda step: self.x, "rows", 4, stride), self.x)

    def gather(self):
        got = others(lambda step: self.x, "rep", self.n_y, 2)
        blocks = jnp.zeros((self.n_y,) + self.x.shape, f32)
        for step, block in enumerate([self.x, *got]):
            at = jnp.mod(self.y + step, self.n_y)
            blocks = lax.dynamic_update_index_in_dim(blocks, block, at, 0)
        self.x = blocks.reshape(-1, self.x.shape[1])

    def whole(self):
        other = from_core(self.x)
        halves = [self.x, other], [other, self.x]
        return jnp.where(self.core == 0, *(jnp.concatenate(h) for h in halves))

    def after(self, *earlier):
        self.x = jnp.where(never(*earlier), 0.0, self.x)


def total(*terms):
    return sum(x.astype(f32) for x in terms).astype(bf16)


def widened(x, size, at):
    return jnp.pad(x, ((at, size - at - x.shape[0]), (0, 0), (0, 0)))


def scatter(mine, other, own, core, steps):
    half = own // 2
    cut = 3 * half
    last = total(mine[0], from_core(other[0]))
    middle = from_core(tied(other[1], last[:1, :8], steps.x[:1, :8]))
    last_up = moved(last[:cut], NEXT_UP, back=True)
    last_down = moved(last[cut:], NEXT_DOWN, back=True)
    first = from_core(tied(other[2], last[:1, :8], steps.x[:1, :8]))
    steps.after(last_up, last_down)
    steps.scatter()
    along = core == 0
    zero = jnp.zeros((), bf16)
    to_up = jnp.where(along, widened(last_up, 2 * cut, 0), zero)
    to_down = jnp.where(along, widened(last_down, 2 * cut, cut), zero)
    next_up = total(mine[1][: 2 * cut], middle[: 2 * cut], to_up)
    next_down = total(mine[1][2 * cut :], middle[2 * cut :], to_down)
    next_up, next_down = moved(next_up, NEXT_UP, back=True), moved(next_down, NEXT_DOWN, back=True)
    far = [jnp.where(along, zero, x[:own]) for x in (last_up, last_down)]
    far = total(mine[2][:own], first[:own], *far)
    half_up = moved(far[:half], HALF_UP, back=True)
    half_down = moved(far[half:], HALF_DOWN, back=True)
    steps.after(half_up, half_down)
    steps.sum_rows(1)
    steps.sum_rows(4)
    none = never(steps.x)
    steps.gather()

    def near(k):
        at = slice(k * own, (k + 1) * own)
        return [mine[2][own:][at], first[own:][at], next_up[at], next_down[at]]

    up = total(*near(1), jnp.where(none, zero, widened(half_up, own, 0)))
    down = total(*near(2), jnp.where(none, zero, widened(half_down, own, half)))
    ends = moved(up, FIRST_UP, back=True), moved(down, FIRST_DOWN, back=True)
    return total(*near(0), *ends)


def local(features, weight, tile_values, tile_cols, tile_live, cotangent):
    n_rows, n_rep = lax.axis_size("rows"), lax.axis_size("rep")
    rep = lax.axis_index("rep")
    node_dev, width = features.shape
    tile = tile_values.shape[2]
    own = node_dev // tile
    group_tiles = own * n_rep
    core = rep % 2
    plans = [layout(own, c) for c in range(2)]
    groups = [len(keys) for keys in plans[0]]
    table = np.zeros((2, 3, n_rep // 2, own), np.int32)
    for c, plan in enumerate(plans):
        for at, key in enumerate(sum(plan, [])):
            if key:
                table[(c, *key)] = at
    place = jnp.mod(tile_cols // group_tiles - lax.axis_index("rows") + 1, n_rows)
    inner = tile_cols % group_tiles
    owner = inner // own
    dy = jnp.mod(owner // 2 - rep // 2, n_rep // 2)
    key = (((owner % 2) * 3 + place) * (n_rep // 2) + dy) * own + inner % own
    hit = key[:, :, None] == jnp.arange(table.size, dtype=jnp.int32)
    at = jnp.sum(jnp.where(hit, jnp.asarray(table.reshape(-1)), 0), axis=2)
    idx = jnp.mod(owner + rep, 2) * sum(groups) + at
    cnt = jnp.sum(tile_live, axis=1)

    parts = gather(features, core)
    output, term, *grads = layer(idx, cnt, tile_values, parts, weight, cotangent, groups)
    steps = Steps(term, core, rep // 2)
    grad = scatter(grads[: len(groups)], grads[len(groups) :], own, core, steps)
    weight_grad = steps.whole()
    feature_grad = jnp.swapaxes(grad, 1, 2).reshape(node_dev, width)
    return (output, feature_grad, weight_grad)


def solution(mesh):
    placed = (
        P(("rows", "rep"), None),
        P(),
        P(("rows", "rep"), None, None, None),
        P(("rows", "rep"), None),
        P(("rows", "rep"), None),
        P(("rows", "rep"), None),
    )
    return jax.shard_map(
        local,
        mesh=mesh,
        in_specs=placed,
        out_specs=(P(("rows", "rep"), None), P(("rows", "rep"), None), P()),
        check_vma=False,
    )
```

```python
import functools

import jax
import jax.numpy as jnp
import numpy as np
from jax import lax
from jax.experimental import pallas as pl
from jax.experimental.pallas import tpu as pltpu
from jax.sharding import PartitionSpec as P

bf16, f32 = jnp.bfloat16, jnp.float32

FWD_SLOTS = 24
BWD_SLOTS = 12
STAGES = 8
CHUNK = 8


def layout(own, core):
    half = own // 2

    def shards(*keys):
        return [(p, dy, i) for p, dy in keys for i in range(own)]

    if core == 0:
        last = shards((1, 2), (0, 2), (2, 2))
        middle = shards((1, 1), (0, 1), (2, 1), (1, 3), (0, 3), (2, 3))
        first = [None] * own + shards((1, 0), (0, 0), (2, 0))
    else:
        last = shards((0, 2)) + [None] * half + shards((2, 2)) + [None] * half
        middle = shards((0, 0), (0, 1), (0, 3), (2, 0), (2, 1), (2, 3))
        first = shards((1, 2), (1, 0), (1, 1), (1, 3))
    return last, middle, first


def kernel(n_in, n_out, idx, cnt, values, *refs):
    parts = refs[:n_in]
    w_ref, cot_ref, out_ref, wg_ref = refs[n_in : n_in + 4]
    outs = refs[n_in + 4 : n_in + 4 + n_out]
    a_ref, win, acc, stage, in_sem, a_sem, out_sem = refs[n_in + 4 + n_out :]
    n_tiles, _, tile, _ = a_ref.shape
    width = w_ref.shape[0]
    copies, row = [], 0
    for k, part in enumerate(parts):
        rows = part.shape[0]
        copies.append(pltpu.make_async_copy(part, win.at[pl.ds(row, rows)], in_sem.at[k]))
        row += rows
    blocks = [pltpu.make_async_copy(values.at[t], a_ref.at[t], a_sem.at[t]) for t in range(n_tiles)]
    for copy in copies + blocks:
        copy.start()
    wg_ref[...] = jnp.zeros_like(wg_ref)

    def zero(i, _):
        acc[pl.ds(i * 8, 8)] = jnp.zeros((8,) + acc.shape[1:], f32)
        return 0

    lax.fori_loop(0, acc.shape[0] // 8, zero, 0)
    for copy in copies:
        copy.wait()

    def row_tile(t, _):
        pltpu.make_async_copy(values.at[t], a_ref.at[t], a_sem.at[t]).wait()
        n = cnt[t]

        def lanes(k0, count):
            got = []
            for j in range(count):
                a = a_ref[t, k0 + j]
                got.append(jnp.where(k0 + j < n, a, jnp.zeros_like(a)))
            return jnp.concatenate(got, axis=1)

        def forward(i, af):
            k0 = i * FWD_SLOTS
            rows = [
                win[pl.ds(pl.multiple_of(idx[t, k0 + j] * tile, tile), tile), :]
                for j in range(FWD_SLOTS)
            ]
            return af + jnp.dot(
                lanes(k0, FWD_SLOTS), jnp.concatenate(rows, axis=0), preferred_element_type=f32
            )

        at = pl.ds(pl.multiple_of(t * tile, tile), tile)
        trips = (n + FWD_SLOTS - 1) // FWD_SLOTS
        af = lax.fori_loop(0, trips, forward, jnp.zeros((tile, width), f32)).astype(bf16)
        pre = jnp.dot(af, w_ref[...], preferred_element_type=f32)
        sig = jax.nn.sigmoid(pre)
        out_ref[at, :] = (pre * sig).astype(bf16)
        g = (cot_ref[at, :].astype(f32) * sig * (1.0 + pre * (1.0 - sig))).astype(bf16)
        wg_ref[...] += lax.dot_general(
            af, g, (((0,), (0,)), ((), ())), preferred_element_type=f32
        )
        gwt = lax.dot_general(
            w_ref[...], g, (((1,), (1,)), ((), ())), preferred_element_type=f32
        ).astype(bf16)

        def backward(i, _):
            k0 = i * BWD_SLOTS
            r = jnp.dot(gwt, lanes(k0, BWD_SLOTS), preferred_element_type=f32)
            for j in range(BWD_SLOTS):
                acc[idx[t, k0 + j]] += r[:, j * tile : (j + 1) * tile]
            return 0

        lax.fori_loop(0, (n + BWD_SLOTS - 1) // BWD_SLOTS, backward, 0)
        return 0

    lax.fori_loop(0, n_tiles, row_tile, 0)
    stages, chunk = stage.shape[:2]

    def copy(slot, out, at):
        return pltpu.make_async_copy(stage.at[slot], out.at[pl.ds(at, chunk)], out_sem.at[slot])

    done = 0
    for out in outs:
        steps = out.shape[0] // chunk

        def emit(i, _, out=out, done=done):
            number = done + i
            slot = lax.rem(number, stages)

            @pl.when(number >= stages)
            def _():
                copy(slot, out, 0).wait()

            stage[slot] = acc[pl.ds(number * chunk, chunk)].astype(bf16)
            copy(slot, out, i * chunk).start()
            return 0

        lax.fori_loop(0, steps, emit, 0)
        done += steps
    for slot in range(stages):
        copy(slot, outs[0], 0).wait()


def layer(idx, cnt, tile_values, parts, weight, cotangent, groups):
    nt, _, tile, _ = tile_values.shape
    width = weight.shape[0]
    n_win = 2 * sum(groups)
    smem = pl.BlockSpec(memory_space=pltpu.SMEM)
    vmem = pl.BlockSpec(memory_space=pltpu.VMEM)
    anywhere = pl.BlockSpec(memory_space=pl.ANY)
    return pl.pallas_call(
        functools.partial(kernel, len(parts), 2 * len(groups)),
        in_specs=[smem, smem] + [anywhere] * (1 + len(parts)) + [vmem, vmem],
        out_specs=[vmem, vmem] + [anywhere] * (2 * len(groups)),
        scratch_shapes=[
            pltpu.VMEM(tile_values.shape, bf16),
            pltpu.VMEM((n_win * tile, width), bf16),
            pltpu.VMEM((n_win, width, tile), f32),
            pltpu.VMEM((STAGES, CHUNK, width, tile), bf16),
            pltpu.SemaphoreType.DMA((len(parts),)),
            pltpu.SemaphoreType.DMA((nt,)),
            pltpu.SemaphoreType.DMA((STAGES,)),
        ],
        out_shape=[
            jax.ShapeDtypeStruct((nt * tile, width), bf16),
            jax.ShapeDtypeStruct((width, width), f32),
        ]
        + [jax.ShapeDtypeStruct((g, width, tile), bf16) for _ in range(2) for g in groups],
        compiler_params=pltpu.CompilerParams(vmem_limit_bytes=60 * 2**20),
        cost_estimate=pl.CostEstimate(
            flops=4 * tile_values.size * width,
            bytes_accessed=6 * tile_values.size,
            transcendentals=0,
        ),
    )(idx, cnt, tile_values, *parts, weight, cotangent)


def tied(x, *earlier):
    return pl.pallas_call(
        lambda *refs: None,
        in_specs=[pl.BlockSpec(memory_space=pl.ANY)] * (1 + len(earlier)),
        out_specs=pl.BlockSpec(memory_space=pl.ANY),
        out_shape=jax.ShapeDtypeStruct(x.shape, x.dtype),
        input_output_aliases={0: 0},
    )(x, *earlier)


def near(group, rep, axis, step, n_rows, n_rep):
    if axis == "z":
        return (group + step) % n_rows * n_rep + rep
    return group * n_rep + (rep + 2 * step) % n_rep


def moved(x, moves, back=False):
    n_rows, n_rep = lax.axis_size("rows"), lax.axis_size("rep")
    pairs = []
    for group in range(n_rows):
        for rep in range(n_rep):
            if moves[rep % 2]:
                source = near(group, rep, *moves[rep % 2], n_rows, n_rep)
                pairs.append((source, group * n_rep + rep))
    if back:
        pairs = [(target, source) for source, target in pairs]
    return lax.ppermute(x, ("rows", "rep"), pairs)


FIRST_UP, FIRST_DOWN = (("z", -1), ("y", 1)), (("z", 1), ("y", -1))
HALF_UP, HALF_DOWN = (None, ("y", 1)), (None, ("y", -1))
NEXT_UP, NEXT_DOWN = (("y", 1), ("z", -1)), (("y", -1), ("z", 1))


def from_core(x):
    return lax.ppermute(x, "rep", [(i, i ^ 1) for i in range(lax.axis_size("rep"))])


def gather(features, core):
    rows = features.shape[0]
    half = rows // 2
    up, down = moved(features, FIRST_UP), moved(features, FIRST_DOWN)
    near3 = jnp.concatenate([features, up, down])
    far = jnp.concatenate([moved(up[:half], HALF_UP), moved(down[half:], HALF_DOWN)])
    up, down = moved(near3, NEXT_UP), moved(near3, NEXT_DOWN)
    crossing = jnp.concatenate([far, far[:half]])
    swapped = from_core(near3)
    swapped_far = from_core(far)
    to_up = jnp.where(core == 0, up[: 3 * half], crossing)
    to_down = jnp.where(core == 0, down[3 * half :], crossing)
    last_up = moved(tied(to_up, swapped, swapped_far), NEXT_UP)
    last_down = moved(to_down, NEXT_DOWN)
    mine = [last_up, last_down, up, down]
    return mine + [far, near3] + [from_core(x) for x in mine] + [swapped_far, swapped]


class Steps:
    def __init__(self, term, core):
        height = term.shape[0] // 2
        low, high = term[:height], term[height:]
        self.x = jnp.where(core == 0, low, high) + from_core(jnp.where(core == 0, high, low))
        self.core = core
        self.left = [
            (axis, bit)
            for axis, first in (("rep", 2), ("rows", 1))
            for bit in (1 << k for k in range(10))
            if first <= bit < lax.axis_size(axis)
        ]

    def go(self, count):
        for axis, bit in self.left[:count]:
            pairs = [(i, i ^ bit) for i in range(lax.axis_size(axis))]
            rounded = lax.reduce_precision(self.x, 8, 7)
            self.x = rounded + lax.ppermute(rounded.astype(bf16), axis, pairs).astype(f32)
        self.left = self.left[count:]

    def after(self, *earlier):
        self.x = tied(self.x, *earlier)

    def whole(self):
        self.go(len(self.left))
        other = from_core(self.x)
        halves = [self.x, other], [other, self.x]
        return jnp.where(self.core == 0, *(jnp.concatenate(h) for h in halves))


def total(*terms):
    return sum(x.astype(f32) for x in terms).astype(bf16)


def widened(x, size, at):
    return jnp.pad(x, ((at, size - at - x.shape[0]), (0, 0), (0, 0)))


def scatter(mine, other, own, core, steps):
    half = own // 2
    cut = 3 * half
    last = total(mine[0], from_core(other[0]))
    middle = from_core(tied(other[1], last[:1, :8], steps.x[:1, :8]))
    last_up = moved(last[:cut], NEXT_UP, back=True)
    last_down = moved(last[cut:], NEXT_DOWN, back=True)
    first = from_core(tied(other[2], last[:1, :8], steps.x[:1, :8]))
    steps.go(2)
    along = core == 0
    zero = jnp.zeros((), bf16)
    to_up = jnp.where(along, widened(last_up, 2 * cut, 0), zero)
    to_down = jnp.where(along, widened(last_down, 2 * cut, cut), zero)
    next_up = total(mine[1][: 2 * cut], middle[: 2 * cut], to_up)
    next_down = total(mine[1][2 * cut :], middle[2 * cut :], to_down)
    next_up = moved(tied(next_up, steps.x), NEXT_UP, back=True)
    next_down = moved(next_down, NEXT_DOWN, back=True)
    far = [jnp.where(along, zero, x[:own]) for x in (last_up, last_down)]
    far = total(mine[2][:own], first[:own], *far)
    half_up = moved(far[:half], HALF_UP, back=True)
    half_down = moved(far[half:], HALF_DOWN, back=True)
    steps.go(1)
    steps.after(half_up[:1, :8], half_down[:1, :8])
    steps.go(2)

    def near(k):
        at = slice(k * own, (k + 1) * own)
        return [mine[2][own:][at], first[own:][at], next_up[at], next_down[at]]

    up = tied(total(*near(1), widened(half_up, own, 0)), steps.x)
    down = total(*near(2), widened(half_down, own, half))
    ends = moved(up, FIRST_UP, back=True), moved(down, FIRST_DOWN, back=True)
    return total(*near(0), *ends)


def local(features, weight, tile_values, tile_cols, tile_live, cotangent):
    n_rows, n_rep = lax.axis_size("rows"), lax.axis_size("rep")
    rep = lax.axis_index("rep")
    node_dev, width = features.shape
    tile = tile_values.shape[2]
    own = node_dev // tile
    group_tiles = own * n_rep
    core = rep % 2
    plans = [layout(own, c) for c in range(2)]
    groups = [len(keys) for keys in plans[0]]
    table = np.zeros((2, 3, n_rep // 2, own), np.int32)
    for c, plan in enumerate(plans):
        for at, key in enumerate(sum(plan, [])):
            if key:
                table[(c, *key)] = at
    place = jnp.mod(tile_cols // group_tiles - lax.axis_index("rows") + 1, n_rows)
    inner = tile_cols % group_tiles
    owner = inner // own
    dy = jnp.mod(owner // 2 - rep // 2, n_rep // 2)
    key = (((owner % 2) * 3 + place) * (n_rep // 2) + dy) * own + inner % own
    hit = key[:, :, None] == jnp.arange(table.size, dtype=jnp.int32)
    at = jnp.sum(jnp.where(hit, jnp.asarray(table.reshape(-1)), 0), axis=2)
    idx = jnp.mod(owner + rep, 2) * sum(groups) + at
    cnt = jnp.sum(tile_live, axis=1)

    parts = gather(features, core)
    output, term, *grads = layer(idx, cnt, tile_values, parts, weight, cotangent, groups)
    steps = Steps(term, core)
    grad = scatter(grads[: len(groups)], grads[len(groups) :], own, core, steps)
    weight_grad = steps.whole()
    feature_grad = jnp.swapaxes(grad, 1, 2).reshape(node_dev, width)
    return (output, feature_grad, weight_grad)


def solution(mesh):
    placed = (
        P(("rows", "rep"), None),
        P(),
        P(("rows", "rep"), None, None, None),
        P(("rows", "rep"), None),
        P(("rows", "rep"), None),
        P(("rows", "rep"), None),
    )
    return jax.shard_map(
        local,
        mesh=mesh,
        in_specs=placed,
        out_specs=(P(("rows", "rep"), None), P(("rows", "rep"), None), P()),
        check_vma=False,
    )
```

```python
import functools

import jax
import jax.numpy as jnp
import numpy as np
from jax import lax
from jax.experimental import pallas as pl
from jax.experimental.pallas import tpu as pltpu
from jax.sharding import PartitionSpec as P

bf16, f32 = jnp.bfloat16, jnp.float32

FWD_SLOTS = 24
BWD_SLOTS = 24
STAGES = 8
CHUNK = 8


def layout(own, core):
    half = own // 2

    def shards(*keys):
        return [(p, dy, i) for p, dy in keys for i in range(own)]

    if core == 0:
        last = shards((1, 2), (0, 2), (2, 2))
        middle = shards((1, 1), (0, 1), (2, 1), (1, 3), (0, 3), (2, 3))
        first = [None] * own + shards((1, 0), (0, 0), (2, 0))
    else:
        last = shards((0, 2)) + [None] * half + shards((2, 2)) + [None] * half
        middle = shards((0, 0), (0, 1), (0, 3), (2, 0), (2, 1), (2, 3))
        first = shards((1, 2), (1, 0), (1, 1), (1, 3))
    return last, middle, first


def kernel(n_in, n_out, idx, cnt, values, *refs):
    parts = refs[:n_in]
    w_ref, cot_ref, out_ref, wg_ref = refs[n_in : n_in + 4]
    outs = refs[n_in + 4 : n_in + 4 + n_out]
    a_ref, win, acc, stage, in_sem, a_sem, out_sem = refs[n_in + 4 + n_out :]
    n_tiles, _, tile, _ = a_ref.shape
    width = w_ref.shape[0]
    copies, row = [], 0
    for k, part in enumerate(parts):
        rows = part.shape[0]
        copies.append(pltpu.make_async_copy(part, win.at[pl.ds(row, rows)], in_sem.at[k]))
        row += rows
    blocks = [pltpu.make_async_copy(values.at[t], a_ref.at[t], a_sem.at[t]) for t in range(n_tiles)]
    for copy in copies + blocks:
        copy.start()
    wg_ref[...] = jnp.zeros_like(wg_ref)

    def zero(i, _):
        acc[pl.ds(i * 8, 8)] = jnp.zeros((8,) + acc.shape[1:], f32)
        return 0

    lax.fori_loop(0, acc.shape[0] // 8, zero, 0)
    for copy in copies:
        copy.wait()

    def row_tile(t, _):
        pltpu.make_async_copy(values.at[t], a_ref.at[t], a_sem.at[t]).wait()
        n = cnt[t]

        def lanes(k0, count):
            got = []
            for j in range(count):
                a = a_ref[t, k0 + j]
                got.append(jnp.where(k0 + j < n, a, jnp.zeros_like(a)))
            return jnp.concatenate(got, axis=1)

        def forward(i, af):
            k0 = i * FWD_SLOTS
            rows = [
                win[pl.ds(pl.multiple_of(idx[t, k0 + j] * tile, tile), tile), :]
                for j in range(FWD_SLOTS)
            ]
            return af + jnp.dot(
                lanes(k0, FWD_SLOTS), jnp.concatenate(rows, axis=0), preferred_element_type=f32
            )

        at = pl.ds(pl.multiple_of(t * tile, tile), tile)
        trips = (n + FWD_SLOTS - 1) // FWD_SLOTS
        af = lax.fori_loop(0, trips, forward, jnp.zeros((tile, width), f32)).astype(bf16)
        pre = jnp.dot(af, w_ref[...], preferred_element_type=f32)
        sig = jax.nn.sigmoid(pre)
        out_ref[at, :] = (pre * sig).astype(bf16)
        g = (cot_ref[at, :].astype(f32) * sig * (1.0 + pre * (1.0 - sig))).astype(bf16)
        wg_ref[...] += lax.dot_general(
            af, g, (((0,), (0,)), ((), ())), preferred_element_type=f32
        )
        gwt = lax.dot_general(
            w_ref[...], g, (((1,), (1,)), ((), ())), preferred_element_type=f32
        ).astype(bf16)

        def backward(i, _):
            k0 = i * BWD_SLOTS
            r = jnp.dot(gwt, lanes(k0, BWD_SLOTS), preferred_element_type=f32)
            for j in range(BWD_SLOTS):
                acc[idx[t, k0 + j]] += r[:, j * tile : (j + 1) * tile]
            return 0

        lax.fori_loop(0, (n + BWD_SLOTS - 1) // BWD_SLOTS, backward, 0)
        return 0

    lax.fori_loop(0, n_tiles, row_tile, 0)
    stages, chunk = stage.shape[:2]

    def copy(slot, out, at):
        return pltpu.make_async_copy(stage.at[slot], out.at[pl.ds(at, chunk)], out_sem.at[slot])

    done = 0
    for out in outs:
        steps = out.shape[0] // chunk

        def emit(i, _, out=out, done=done):
            number = done + i
            slot = lax.rem(number, stages)

            @pl.when(number >= stages)
            def _():
                copy(slot, out, 0).wait()

            stage[slot] = acc[pl.ds(number * chunk, chunk)].astype(bf16)
            copy(slot, out, i * chunk).start()
            return 0

        lax.fori_loop(0, steps, emit, 0)
        done += steps
    for slot in range(stages):
        copy(slot, outs[0], 0).wait()


def layer(idx, cnt, tile_values, parts, weight, cotangent, groups):
    nt, _, tile, _ = tile_values.shape
    width = weight.shape[0]
    n_win = 2 * sum(groups)
    smem = pl.BlockSpec(memory_space=pltpu.SMEM)
    vmem = pl.BlockSpec(memory_space=pltpu.VMEM)
    anywhere = pl.BlockSpec(memory_space=pl.ANY)
    return pl.pallas_call(
        functools.partial(kernel, len(parts), 2 * len(groups)),
        in_specs=[smem, smem] + [anywhere] * (1 + len(parts)) + [vmem, vmem],
        out_specs=[vmem, vmem] + [anywhere] * (2 * len(groups)),
        scratch_shapes=[
            pltpu.VMEM(tile_values.shape, bf16),
            pltpu.VMEM((n_win * tile, width), bf16),
            pltpu.VMEM((n_win, width, tile), f32),
            pltpu.VMEM((STAGES, CHUNK, width, tile), bf16),
            pltpu.SemaphoreType.DMA((len(parts),)),
            pltpu.SemaphoreType.DMA((nt,)),
            pltpu.SemaphoreType.DMA((STAGES,)),
        ],
        out_shape=[
            jax.ShapeDtypeStruct((nt * tile, width), bf16),
            jax.ShapeDtypeStruct((width, width), f32),
        ]
        + [jax.ShapeDtypeStruct((g, width, tile), bf16) for _ in range(2) for g in groups],
        compiler_params=pltpu.CompilerParams(vmem_limit_bytes=60 * 2**20),
        cost_estimate=pl.CostEstimate(
            flops=4 * tile_values.size * width,
            bytes_accessed=6 * tile_values.size,
            transcendentals=0,
        ),
    )(idx, cnt, tile_values, *parts, weight, cotangent)


def tied(x, *earlier):
    return pl.pallas_call(
        lambda *refs: None,
        in_specs=[pl.BlockSpec(memory_space=pl.ANY)] * (1 + len(earlier)),
        out_specs=pl.BlockSpec(memory_space=pl.ANY),
        out_shape=jax.ShapeDtypeStruct(x.shape, x.dtype),
        input_output_aliases={0: 0},
    )(x, *earlier)


def near(group, rep, axis, step, n_rows, n_rep):
    if axis == "z":
        return (group + step) % n_rows * n_rep + rep
    return group * n_rep + (rep + 2 * step) % n_rep


def moved(x, moves, back=False):
    n_rows, n_rep = lax.axis_size("rows"), lax.axis_size("rep")
    pairs = []
    for group in range(n_rows):
        for rep in range(n_rep):
            if moves[rep % 2]:
                source = near(group, rep, *moves[rep % 2], n_rows, n_rep)
                pairs.append((source, group * n_rep + rep))
    if back:
        pairs = [(target, source) for source, target in pairs]
    return lax.ppermute(x, ("rows", "rep"), pairs)


FIRST_UP, FIRST_DOWN = (("z", -1), ("y", 1)), (("z", 1), ("y", -1))
HALF_UP, HALF_DOWN = (None, ("y", 1)), (None, ("y", -1))
NEXT_UP, NEXT_DOWN = (("y", 1), ("z", -1)), (("y", -1), ("z", 1))


def from_core(x):
    return lax.ppermute(x, "rep", [(i, i ^ 1) for i in range(lax.axis_size("rep"))])


def gather(features, core):
    rows = features.shape[0]
    half = rows // 2
    up, down = moved(features, FIRST_UP), moved(features, FIRST_DOWN)
    near3 = jnp.concatenate([features, up, down])
    far = jnp.concatenate([moved(up[:half], HALF_UP), moved(down[half:], HALF_DOWN)])
    up, down = moved(near3, NEXT_UP), moved(near3, NEXT_DOWN)
    crossing = jnp.concatenate([far, far[:half]])
    swapped = from_core(near3)
    swapped_far = from_core(far)
    to_up = jnp.where(core == 0, up[: 3 * half], crossing)
    to_down = jnp.where(core == 0, down[3 * half :], crossing)
    last_up = moved(tied(to_up, swapped[:8], swapped_far[:8]), NEXT_UP)
    last_down = moved(to_down, NEXT_DOWN)
    mine = [last_up, last_down, up, down]
    return mine + [far, near3] + [from_core(x) for x in mine] + [swapped_far, swapped]


class Steps:
    def __init__(self, term, core):
        height = term.shape[0] // 2
        low, high = term[:height], term[height:]
        self.mine, self.other = jnp.where(core == 0, low, high), jnp.where(core == 0, high, low)
        self.core = core
        self.left = [
            (axis, bit)
            for axis, first in (("rep", 2), ("rows", 1))
            for bit in (1 << k for k in range(10))
            if first <= bit < lax.axis_size(axis)
        ]

    def begin(self, *earlier):
        self.x = self.mine + from_core(tied(self.other, *earlier))

    def go(self, count):
        for axis, bit in self.left[:count]:
            pairs = [(i, i ^ bit) for i in range(lax.axis_size(axis))]
            rounded = lax.reduce_precision(self.x, 8, 7)
            self.x = rounded + lax.ppermute(rounded.astype(bf16), axis, pairs).astype(f32)
        self.left = self.left[count:]

    def after(self, *earlier):
        self.x = tied(self.x, *earlier)

    def whole(self):
        self.go(len(self.left))
        other = from_core(self.x)
        halves = [self.x, other], [other, self.x]
        return jnp.where(self.core == 0, *(jnp.concatenate(h) for h in halves))


def total(*terms):
    return sum(x.astype(f32) for x in terms).astype(bf16)


def widened(x, size, at):
    return jnp.pad(x, ((at, size - at - x.shape[0]), (0, 0), (0, 0)))


def scatter(mine, other, own, core, steps):
    half = own // 2
    cut = 3 * half
    last = total(mine[0], from_core(other[0]))
    begun = last[:1, :8]
    middle = from_core(tied(other[1], begun))
    last_up = moved(last[:cut], NEXT_UP, back=True)
    last_down = moved(last[cut:], NEXT_DOWN, back=True)
    first = from_core(tied(other[2], begun))
    steps.begin(begun)
    steps.go(1)
    along = core == 0
    zero = jnp.zeros((), bf16)
    to_up = jnp.where(along, widened(last_up, 2 * cut, 0), zero)
    to_down = jnp.where(along, widened(last_down, 2 * cut, cut), zero)
    next_up = total(mine[1][: 2 * cut], middle[: 2 * cut], to_up)
    next_down = total(mine[1][2 * cut :], middle[2 * cut :], to_down)
    next_up = moved(tied(next_up, steps.x), NEXT_UP, back=True)
    next_down = moved(next_down, NEXT_DOWN, back=True)
    far = [jnp.where(along, zero, x[:own]) for x in (last_up, last_down)]
    far = total(mine[2][:own], first[:own], *far)
    half_up = moved(far[:half], HALF_UP, back=True)
    half_down = moved(far[half:], HALF_DOWN, back=True)
    steps.go(1)
    steps.after(half_up[:1, :8], half_down[:1, :8])
    steps.go(2)

    def near(k):
        at = slice(k * own, (k + 1) * own)
        return [mine[2][own:][at], first[own:][at], next_up[at], next_down[at]]

    up = tied(total(*near(1), widened(half_up, own, 0)), steps.x)
    down = total(*near(2), widened(half_down, own, half))
    steps.after(down[:1, :8])
    ends = moved(up, FIRST_UP, back=True), moved(down, FIRST_DOWN, back=True)
    return total(*near(0), *ends)


def local(features, weight, tile_values, tile_cols, tile_live, cotangent):
    n_rows, n_rep = lax.axis_size("rows"), lax.axis_size("rep")
    rep = lax.axis_index("rep")
    node_dev, width = features.shape
    tile = tile_values.shape[2]
    own = node_dev // tile
    group_tiles = own * n_rep
    core = rep % 2
    plans = [layout(own, c) for c in range(2)]
    groups = [len(keys) for keys in plans[0]]
    table = np.zeros((2, 3, n_rep // 2, own), np.int32)
    for c, plan in enumerate(plans):
        for at, key in enumerate(sum(plan, [])):
            if key:
                table[(c, *key)] = at
    place = jnp.mod(tile_cols // group_tiles - lax.axis_index("rows") + 1, n_rows)
    inner = tile_cols % group_tiles
    owner = inner // own
    dy = jnp.mod(owner // 2 - rep // 2, n_rep // 2)
    key = (((owner % 2) * 3 + place) * (n_rep // 2) + dy) * own + inner % own
    hit = key[:, :, None] == jnp.arange(table.size, dtype=jnp.int32)
    at = jnp.sum(jnp.where(hit, jnp.asarray(table.reshape(-1)), 0), axis=2)
    idx = jnp.mod(owner + rep, 2) * sum(groups) + at
    cnt = jnp.sum(tile_live, axis=1)

    parts = gather(features, core)
    output, term, *grads = layer(idx, cnt, tile_values, parts, weight, cotangent, groups)
    steps = Steps(term, core)
    grad = scatter(grads[: len(groups)], grads[len(groups) :], own, core, steps)
    weight_grad = steps.whole()
    feature_grad = jnp.swapaxes(grad, 1, 2).reshape(node_dev, width)
    return (output, feature_grad, weight_grad)


def solution(mesh):
    placed = (
        P(("rows", "rep"), None),
        P(),
        P(("rows", "rep"), None, None, None),
        P(("rows", "rep"), None),
        P(("rows", "rep"), None),
        P(("rows", "rep"), None),
    )
    return jax.shard_map(
        local,
        mesh=mesh,
        in_specs=placed,
        out_specs=(P(("rows", "rep"), None), P(("rows", "rep"), None), P()),
        check_vma=False,
    )
```

```python
import functools

import jax
import jax.numpy as jnp
import numpy as np
from jax import lax
from jax.experimental import pallas as pl
from jax.experimental.pallas import tpu as pltpu
from jax.sharding import PartitionSpec as P

bf16, f32 = jnp.bfloat16, jnp.float32

FWD_SLOTS = 24
BWD_SLOTS = 24
STAGES = 8
CHUNK = 8


def layout(own, core):
    half = own // 2

    def shards(*keys):
        return [(p, dy, i) for p, dy in keys for i in range(own)]

    if core == 0:
        last = shards((1, 2), (0, 2), (2, 2))
        middle = shards((1, 1), (0, 1), (2, 1), (1, 3), (0, 3), (2, 3))
        first = [None] * own + shards((1, 0), (0, 0), (2, 0))
    else:
        last = shards((0, 2)) + [None] * half + shards((2, 2)) + [None] * half
        middle = shards((0, 0), (0, 1), (0, 3), (2, 0), (2, 1), (2, 3))
        first = shards((1, 2), (1, 0), (1, 1), (1, 3))
    return last, middle, first


def kernel(n_in, n_out, idx, cnt, values, *refs):
    parts = refs[:n_in]
    w_ref, cot_ref, out_ref, wg_ref = refs[n_in : n_in + 4]
    outs = refs[n_in + 4 : n_in + 4 + n_out]
    a_ref, win, acc, stage, in_sem, a_sem, out_sem = refs[n_in + 4 + n_out :]
    n_tiles, _, tile, _ = a_ref.shape
    width = w_ref.shape[0]
    copies, row = [], 0
    for k, part in enumerate(parts):
        rows = part.shape[0]
        copies.append(pltpu.make_async_copy(part, win.at[pl.ds(row, rows)], in_sem.at[k]))
        row += rows
    blocks = [pltpu.make_async_copy(values.at[t], a_ref.at[t], a_sem.at[t]) for t in range(n_tiles)]
    for copy in copies + blocks:
        copy.start()
    wg_ref[...] = jnp.zeros_like(wg_ref)

    def zero(i, _):
        acc[pl.ds(i * 8, 8)] = jnp.zeros((8,) + acc.shape[1:], f32)
        return 0

    lax.fori_loop(0, acc.shape[0] // 8, zero, 0)
    for copy in copies:
        copy.wait()

    def row_tile(t, _):
        pltpu.make_async_copy(values.at[t], a_ref.at[t], a_sem.at[t]).wait()
        n = cnt[t]

        def lanes(k0, count):
            got = []
            for j in range(count):
                a = a_ref[t, k0 + j]
                got.append(jnp.where(k0 + j < n, a, jnp.zeros_like(a)))
            return jnp.concatenate(got, axis=1)

        def forward(i, af):
            k0 = i * FWD_SLOTS
            rows = [
                win[pl.ds(pl.multiple_of(idx[t, k0 + j] * tile, tile), tile), :]
                for j in range(FWD_SLOTS)
            ]
            return af + jnp.dot(
                lanes(k0, FWD_SLOTS), jnp.concatenate(rows, axis=0), preferred_element_type=f32
            )

        at = pl.ds(pl.multiple_of(t * tile, tile), tile)
        trips = (n + FWD_SLOTS - 1) // FWD_SLOTS
        af = lax.fori_loop(0, trips, forward, jnp.zeros((tile, width), f32)).astype(bf16)
        pre = jnp.dot(af, w_ref[...], preferred_element_type=f32)
        sig = jax.nn.sigmoid(pre)
        out_ref[at, :] = (pre * sig).astype(bf16)
        g = (cot_ref[at, :].astype(f32) * sig * (1.0 + pre * (1.0 - sig))).astype(bf16)
        wg_ref[...] += lax.dot_general(
            af, g, (((0,), (0,)), ((), ())), preferred_element_type=f32
        )
        gwt = lax.dot_general(
            w_ref[...], g, (((1,), (1,)), ((), ())), preferred_element_type=f32
        ).astype(bf16)

        def backward(i, _):
            k0 = i * BWD_SLOTS
            r = jnp.dot(gwt, lanes(k0, BWD_SLOTS), preferred_element_type=f32)
            for j in range(BWD_SLOTS):
                acc[idx[t, k0 + j]] += r[:, j * tile : (j + 1) * tile]
            return 0

        lax.fori_loop(0, (n + BWD_SLOTS - 1) // BWD_SLOTS, backward, 0)
        return 0

    lax.fori_loop(0, n_tiles, row_tile, 0)
    stages, chunk = stage.shape[:2]

    def copy(slot, out, at):
        return pltpu.make_async_copy(stage.at[slot], out.at[pl.ds(at, chunk)], out_sem.at[slot])

    done = 0
    for out in outs:
        steps = out.shape[0] // chunk

        def emit(i, _, out=out, done=done):
            number = done + i
            slot = lax.rem(number, stages)

            @pl.when(number >= stages)
            def _():
                copy(slot, out, 0).wait()

            stage[slot] = acc[pl.ds(number * chunk, chunk)].astype(bf16)
            copy(slot, out, i * chunk).start()
            return 0

        lax.fori_loop(0, steps, emit, 0)
        done += steps
    for slot in range(stages):
        copy(slot, outs[0], 0).wait()


def layer(idx, cnt, tile_values, parts, weight, cotangent, groups):
    nt, _, tile, _ = tile_values.shape
    width = weight.shape[0]
    n_win = 2 * sum(groups)
    smem = pl.BlockSpec(memory_space=pltpu.SMEM)
    vmem = pl.BlockSpec(memory_space=pltpu.VMEM)
    anywhere = pl.BlockSpec(memory_space=pl.ANY)
    return pl.pallas_call(
        functools.partial(kernel, len(parts), 2 * len(groups)),
        in_specs=[smem, smem] + [anywhere] * (1 + len(parts)) + [vmem, vmem],
        out_specs=[vmem, vmem] + [anywhere] * (2 * len(groups)),
        scratch_shapes=[
            pltpu.VMEM(tile_values.shape, bf16),
            pltpu.VMEM((n_win * tile, width), bf16),
            pltpu.VMEM((n_win, width, tile), f32),
            pltpu.VMEM((STAGES, CHUNK, width, tile), bf16),
            pltpu.SemaphoreType.DMA((len(parts),)),
            pltpu.SemaphoreType.DMA((nt,)),
            pltpu.SemaphoreType.DMA((STAGES,)),
        ],
        out_shape=[
            jax.ShapeDtypeStruct((nt * tile, width), bf16),
            jax.ShapeDtypeStruct((width, width), f32),
        ]
        + [jax.ShapeDtypeStruct((g, width, tile), bf16) for _ in range(2) for g in groups],
        compiler_params=pltpu.CompilerParams(vmem_limit_bytes=60 * 2**20),
        cost_estimate=pl.CostEstimate(
            flops=4 * tile_values.size * width,
            bytes_accessed=6 * tile_values.size,
            transcendentals=0,
        ),
    )(idx, cnt, tile_values, *parts, weight, cotangent)


def tied(x, *earlier):
    return pl.pallas_call(
        lambda *refs: None,
        in_specs=[pl.BlockSpec(memory_space=pl.ANY)] * (1 + len(earlier)),
        out_specs=pl.BlockSpec(memory_space=pl.ANY),
        out_shape=jax.ShapeDtypeStruct(x.shape, x.dtype),
        input_output_aliases={0: 0},
    )(x, *earlier)


def near(group, rep, axis, step, n_rows, n_rep):
    if axis == "z":
        return (group + step) % n_rows * n_rep + rep
    return group * n_rep + (rep + 2 * step) % n_rep


def moved(x, moves, back=False):
    n_rows, n_rep = lax.axis_size("rows"), lax.axis_size("rep")
    pairs = []
    for group in range(n_rows):
        for rep in range(n_rep):
            if moves[rep % 2]:
                source = near(group, rep, *moves[rep % 2], n_rows, n_rep)
                pairs.append((source, group * n_rep + rep))
    if back:
        pairs = [(target, source) for source, target in pairs]
    return lax.ppermute(x, ("rows", "rep"), pairs)


FIRST_UP, FIRST_DOWN = (("z", -1), ("y", 1)), (("z", 1), ("y", -1))
HALF_UP, HALF_DOWN = (None, ("y", 1)), (None, ("y", -1))
NEXT_UP, NEXT_DOWN = (("y", 1), ("z", -1)), (("y", -1), ("z", 1))


def from_core(x):
    return lax.ppermute(x, "rep", [(i, i ^ 1) for i in range(lax.axis_size("rep"))])


def gather(features, core):
    rows = features.shape[0]
    half = rows // 2
    up, down = moved(features, FIRST_UP), moved(features, FIRST_DOWN)
    near3 = jnp.concatenate([features, up, down])
    far = jnp.concatenate([moved(up[:half], HALF_UP), moved(down[half:], HALF_DOWN)])
    up, down = moved(near3, NEXT_UP), moved(near3, NEXT_DOWN)
    crossing = jnp.concatenate([far, far[:half]])
    swapped = from_core(near3)
    swapped_far = from_core(far)
    to_up = jnp.where(core == 0, up[: 3 * half], crossing)
    to_down = jnp.where(core == 0, down[3 * half :], crossing)
    last_up = moved(tied(to_up, swapped[:8], swapped_far[:8]), NEXT_UP)
    last_down = moved(to_down, NEXT_DOWN)
    mine = [last_up, last_down, up, down]
    return mine + [far, near3] + [from_core(x) for x in mine] + [swapped_far, swapped]


class Steps:
    def __init__(self, term, core):
        height = term.shape[0] // 2
        low, high = term[:height], term[height:]
        self.mine, self.other = jnp.where(core == 0, low, high), jnp.where(core == 0, high, low)
        self.core = core
        self.left = [
            (axis, bit)
            for axis, first in (("rep", 2), ("rows", 1))
            for bit in (1 << k for k in range(10))
            if first <= bit < lax.axis_size(axis)
        ]

    def begin(self, *earlier):
        self.x = self.mine + from_core(tied(self.other, *earlier))

    def go(self, count):
        for axis, bit in self.left[:count]:
            pairs = [(i, i ^ bit) for i in range(lax.axis_size(axis))]
            rounded = lax.reduce_precision(self.x, 8, 7)
            self.x = rounded + lax.ppermute(rounded.astype(bf16), axis, pairs).astype(f32)
        self.left = self.left[count:]

    def after(self, *earlier):
        self.x = tied(self.x, *earlier)

    def whole(self):
        self.go(len(self.left))
        other = from_core(self.x)
        halves = [self.x, other], [other, self.x]
        return jnp.where(self.core == 0, *(jnp.concatenate(h) for h in halves))


def total(*terms):
    return sum(x.astype(f32) for x in terms).astype(bf16)


def widened(x, size, at):
    return jnp.pad(x, ((at, size - at - x.shape[0]), (0, 0), (0, 0)))


def scatter(mine, other, own, core, steps):
    half = own // 2
    cut = 3 * half
    last = total(mine[0], from_core(other[0]))
    begun = last[:1, :8]
    middle = from_core(tied(other[1], begun))
    last_up = moved(last[:cut], NEXT_UP, back=True)
    last_down = moved(last[cut:], NEXT_DOWN, back=True)
    first = from_core(tied(other[2], begun))
    steps.begin(begun)
    steps.go(1)
    along = core == 0
    zero = jnp.zeros((), bf16)
    to_up = jnp.where(along, widened(last_up, 2 * cut, 0), zero)
    to_down = jnp.where(along, widened(last_down, 2 * cut, cut), zero)
    next_up = total(mine[1][: 2 * cut], middle[: 2 * cut], to_up)
    next_down = total(mine[1][2 * cut :], middle[2 * cut :], to_down)
    next_up = moved(tied(next_up, steps.x), NEXT_UP, back=True)
    next_down = moved(next_down, NEXT_DOWN, back=True)
    far = [jnp.where(along, zero, x[:own]) for x in (last_up, last_down)]
    far = total(mine[2][:own], first[:own], *far)
    half_up = moved(far[:half], HALF_UP, back=True)
    half_down = moved(far[half:], HALF_DOWN, back=True)
    steps.go(1)
    steps.after(half_up[:1, :8], half_down[:1, :8])
    steps.go(3)

    def near(k):
        at = slice(k * own, (k + 1) * own)
        return [mine[2][own:][at], first[own:][at], next_up[at], next_down[at]]

    up = tied(total(*near(1), widened(half_up, own, 0)), steps.x)
    down = total(*near(2), widened(half_down, own, half))
    ends = moved(up, FIRST_UP, back=True), moved(down, FIRST_DOWN, back=True)
    return total(*near(0), *ends)


def local(features, weight, tile_values, tile_cols, tile_live, cotangent):
    n_rows, n_rep = lax.axis_size("rows"), lax.axis_size("rep")
    rep = lax.axis_index("rep")
    node_dev, width = features.shape
    tile = tile_values.shape[2]
    own = node_dev // tile
    group_tiles = own * n_rep
    core = rep % 2
    plans = [layout(own, c) for c in range(2)]
    groups = [len(keys) for keys in plans[0]]
    table = np.zeros((2, 3, n_rep // 2, own), np.int32)
    for c, plan in enumerate(plans):
        for at, key in enumerate(sum(plan, [])):
            if key:
                table[(c, *key)] = at
    place = jnp.mod(tile_cols // group_tiles - lax.axis_index("rows") + 1, n_rows)
    inner = tile_cols % group_tiles
    owner = inner // own
    dy = jnp.mod(owner // 2 - rep // 2, n_rep // 2)
    key = (((owner % 2) * 3 + place) * (n_rep // 2) + dy) * own + inner % own
    hit = key[:, :, None] == jnp.arange(table.size, dtype=jnp.int32)
    at = jnp.sum(jnp.where(hit, jnp.asarray(table.reshape(-1)), 0), axis=2)
    idx = jnp.mod(owner + rep, 2) * sum(groups) + at
    cnt = jnp.sum(tile_live, axis=1)

    parts = gather(features, core)
    output, term, *grads = layer(idx, cnt, tile_values, parts, weight, cotangent, groups)
    steps = Steps(term, core)
    grad = scatter(grads[: len(groups)], grads[len(groups) :], own, core, steps)
    weight_grad = steps.whole()
    feature_grad = jnp.swapaxes(grad, 1, 2).reshape(node_dev, width)
    return (output, feature_grad, weight_grad)


def solution(mesh):
    placed = (
        P(("rows", "rep"), None),
        P(),
        P(("rows", "rep"), None, None, None),
        P(("rows", "rep"), None),
        P(("rows", "rep"), None),
        P(("rows", "rep"), None),
    )
    return jax.shard_map(
        local,
        mesh=mesh,
        in_specs=placed,
        out_specs=(P(("rows", "rep"), None), P(("rows", "rep"), None), P()),
        check_vma=False,
    )
```

```python
import functools

import jax
import jax.numpy as jnp
import numpy as np
from jax import lax
from jax.experimental import pallas as pl
from jax.experimental.pallas import tpu as pltpu
from jax.sharding import PartitionSpec as P

bf16, f32 = jnp.bfloat16, jnp.float32

FWD_SLOTS = 48
BWD_SLOTS = 24
STAGES = 8
CHUNK = 8


def layout(own, core):
    half = own // 2

    def shards(*keys):
        return [(p, dy, i) for p, dy in keys for i in range(own)]

    if core == 0:
        last = shards((1, 2), (0, 2), (2, 2))
        middle = shards((1, 1), (0, 1), (2, 1), (1, 3), (0, 3), (2, 3))
        first = [None] * own + shards((1, 0), (0, 0), (2, 0))
    else:
        last = shards((0, 2)) + [None] * half + shards((2, 2)) + [None] * half
        middle = shards((0, 0), (0, 1), (0, 3), (2, 0), (2, 1), (2, 3))
        first = shards((1, 2), (1, 0), (1, 1), (1, 3))
    return last, middle, first


def kernel(n_in, n_out, idx, cnt, values, *refs):
    parts = refs[:n_in]
    w_ref, cot_ref, out_ref, wg_ref = refs[n_in : n_in + 4]
    outs = refs[n_in + 4 : n_in + 4 + n_out]
    a_ref, win, acc, stage, in_sem, a_sem, out_sem = refs[n_in + 4 + n_out :]
    n_tiles, _, tile, _ = a_ref.shape
    width = w_ref.shape[0]
    copies, row = [], 0
    for k, part in enumerate(parts):
        rows = part.shape[0]
        copies.append(pltpu.make_async_copy(part, win.at[pl.ds(row, rows)], in_sem.at[k]))
        row += rows
    blocks = [pltpu.make_async_copy(values.at[t], a_ref.at[t], a_sem.at[t]) for t in range(n_tiles)]
    for copy in copies + blocks:
        copy.start()
    wg_ref[...] = jnp.zeros_like(wg_ref)

    def zero(i, _):
        acc[pl.ds(i * 8, 8)] = jnp.zeros((8,) + acc.shape[1:], f32)
        return 0

    lax.fori_loop(0, acc.shape[0] // 8, zero, 0)
    for copy in copies:
        copy.wait()

    def row_tile(t, _):
        pltpu.make_async_copy(values.at[t], a_ref.at[t], a_sem.at[t]).wait()
        n = cnt[t]

        def lanes(k0, count):
            got = []
            for j in range(count):
                a = a_ref[t, k0 + j]
                got.append(jnp.where(k0 + j < n, a, jnp.zeros_like(a)))
            return jnp.concatenate(got, axis=1)

        def forward(i, af):
            k0 = i * FWD_SLOTS
            rows = [
                win[pl.ds(pl.multiple_of(idx[t, k0 + j] * tile, tile), tile), :]
                for j in range(FWD_SLOTS)
            ]
            return af + jnp.dot(
                lanes(k0, FWD_SLOTS), jnp.concatenate(rows, axis=0), preferred_element_type=f32
            )

        at = pl.ds(pl.multiple_of(t * tile, tile), tile)
        trips = (n + FWD_SLOTS - 1) // FWD_SLOTS
        af = lax.fori_loop(0, trips, forward, jnp.zeros((tile, width), f32)).astype(bf16)
        pre = jnp.dot(af, w_ref[...], preferred_element_type=f32)
        sig = jax.nn.sigmoid(pre)
        out_ref[at, :] = (pre * sig).astype(bf16)
        g = (cot_ref[at, :].astype(f32) * sig * (1.0 + pre * (1.0 - sig))).astype(bf16)
        wg_ref[...] += lax.dot_general(
            af, g, (((0,), (0,)), ((), ())), preferred_element_type=f32
        )
        gwt = lax.dot_general(
            w_ref[...], g, (((1,), (1,)), ((), ())), preferred_element_type=f32
        ).astype(bf16)

        def backward(i, _):
            k0 = i * BWD_SLOTS
            r = jnp.dot(gwt, lanes(k0, BWD_SLOTS), preferred_element_type=f32)
            for j in range(BWD_SLOTS):
                acc[idx[t, k0 + j]] += r[:, j * tile : (j + 1) * tile]
            return 0

        lax.fori_loop(0, (n + BWD_SLOTS - 1) // BWD_SLOTS, backward, 0)
        return 0

    lax.fori_loop(0, n_tiles, row_tile, 0)
    stages, chunk = stage.shape[:2]

    def copy(slot, out, at):
        return pltpu.make_async_copy(stage.at[slot], out.at[pl.ds(at, chunk)], out_sem.at[slot])

    done = 0
    for out in outs:
        steps = out.shape[0] // chunk

        def emit(i, _, out=out, done=done):
            number = done + i
            slot = lax.rem(number, stages)

            @pl.when(number >= stages)
            def _():
                copy(slot, out, 0).wait()

            stage[slot] = acc[pl.ds(number * chunk, chunk)].astype(bf16)
            copy(slot, out, i * chunk).start()
            return 0

        lax.fori_loop(0, steps, emit, 0)
        done += steps
    for slot in range(stages):
        copy(slot, outs[0], 0).wait()


def layer(idx, cnt, tile_values, parts, weight, cotangent, groups):
    nt, _, tile, _ = tile_values.shape
    width = weight.shape[0]
    n_win = 2 * sum(groups)
    smem = pl.BlockSpec(memory_space=pltpu.SMEM)
    vmem = pl.BlockSpec(memory_space=pltpu.VMEM)
    anywhere = pl.BlockSpec(memory_space=pl.ANY)
    return pl.pallas_call(
        functools.partial(kernel, len(parts), 2 * len(groups)),
        in_specs=[smem, smem] + [anywhere] * (1 + len(parts)) + [vmem, vmem],
        out_specs=[vmem, vmem] + [anywhere] * (2 * len(groups)),
        scratch_shapes=[
            pltpu.VMEM(tile_values.shape, bf16),
            pltpu.VMEM((n_win * tile, width), bf16),
            pltpu.VMEM((n_win, width, tile), f32),
            pltpu.VMEM((STAGES, CHUNK, width, tile), bf16),
            pltpu.SemaphoreType.DMA((len(parts),)),
            pltpu.SemaphoreType.DMA((nt,)),
            pltpu.SemaphoreType.DMA((STAGES,)),
        ],
        out_shape=[
            jax.ShapeDtypeStruct((nt * tile, width), bf16),
            jax.ShapeDtypeStruct((width, width), f32),
        ]
        + [jax.ShapeDtypeStruct((g, width, tile), bf16) for _ in range(2) for g in groups],
        compiler_params=pltpu.CompilerParams(vmem_limit_bytes=60 * 2**20),
        cost_estimate=pl.CostEstimate(
            flops=4 * tile_values.size * width,
            bytes_accessed=6 * tile_values.size,
            transcendentals=0,
        ),
    )(idx, cnt, tile_values, *parts, weight, cotangent)


def tied(x, *earlier):
    return pl.pallas_call(
        lambda *refs: None,
        in_specs=[pl.BlockSpec(memory_space=pl.ANY)] * (1 + len(earlier)),
        out_specs=pl.BlockSpec(memory_space=pl.ANY),
        out_shape=jax.ShapeDtypeStruct(x.shape, x.dtype),
        input_output_aliases={0: 0},
    )(x, *earlier)


def near(group, rep, axis, step, n_rows, n_rep):
    if axis == "z":
        return (group + step) % n_rows * n_rep + rep
    return group * n_rep + (rep + 2 * step) % n_rep


def moved(x, moves, back=False):
    n_rows, n_rep = lax.axis_size("rows"), lax.axis_size("rep")
    pairs = []
    for group in range(n_rows):
        for rep in range(n_rep):
            if moves[rep % 2]:
                source = near(group, rep, *moves[rep % 2], n_rows, n_rep)
                pairs.append((source, group * n_rep + rep))
    if back:
        pairs = [(target, source) for source, target in pairs]
    return lax.ppermute(x, ("rows", "rep"), pairs)


FIRST_UP, FIRST_DOWN = (("z", -1), ("y", 1)), (("z", 1), ("y", -1))
HALF_UP, HALF_DOWN = (None, ("y", 1)), (None, ("y", -1))
NEXT_UP, NEXT_DOWN = (("y", 1), ("z", -1)), (("y", -1), ("z", 1))


def from_core(x):
    return lax.ppermute(x, "rep", [(i, i ^ 1) for i in range(lax.axis_size("rep"))])


def gather(features, core):
    rows = features.shape[0]
    half = rows // 2
    up, down = moved(features, FIRST_UP), moved(features, FIRST_DOWN)
    near3 = jnp.concatenate([features, up, down])
    far = jnp.concatenate([moved(up[:half], HALF_UP), moved(down[half:], HALF_DOWN)])
    up, down = moved(near3, NEXT_UP), moved(near3, NEXT_DOWN)
    crossing = jnp.concatenate([far, far[:half]])
    swapped = from_core(near3)
    swapped_far = from_core(far)
    to_up = jnp.where(core == 0, up[: 3 * half], crossing)
    to_down = jnp.where(core == 0, down[3 * half :], crossing)
    last_up = moved(tied(to_up, swapped[:8], swapped_far[:8]), NEXT_UP)
    last_down = moved(to_down, NEXT_DOWN)
    mine = [last_up, last_down, up, down]
    return mine + [far, near3] + [from_core(x) for x in mine] + [swapped_far, swapped]


class Steps:
    def __init__(self, term, core):
        height = term.shape[0] // 2
        low, high = term[:height], term[height:]
        self.mine = jnp.where(core == 0, low, high)
        self.got = from_core(jnp.where(core == 0, high, low))
        self.core = core
        self.left = [
            (axis, bit)
            for axis, first in (("rep", 2), ("rows", 1))
            for bit in (1 << k for k in range(10))
            if first <= bit < lax.axis_size(axis)
        ]

    def begin(self, *earlier):
        self.x = self.mine + tied(self.got, *earlier)

    def go(self, count):
        for axis, bit in self.left[:count]:
            pairs = [(i, i ^ bit) for i in range(lax.axis_size(axis))]
            rounded = lax.reduce_precision(self.x, 8, 7)
            self.x = rounded + lax.ppermute(rounded.astype(bf16), axis, pairs).astype(f32)
        self.left = self.left[count:]

    def after(self, *earlier):
        self.x = tied(self.x, *earlier)

    def whole(self):
        self.go(len(self.left))
        other = from_core(self.x)
        halves = [self.x, other], [other, self.x]
        return jnp.where(self.core == 0, *(jnp.concatenate(h) for h in halves))


def total(*terms):
    return sum(x.astype(f32) for x in terms).astype(bf16)


def widened(x, size, at):
    return jnp.pad(x, ((at, size - at - x.shape[0]), (0, 0), (0, 0)))


def scatter(mine, other, own, core, steps):
    half = own // 2
    cut = 3 * half
    last = total(mine[0], from_core(other[0]))
    begun = last[:1, :8]
    middle = from_core(tied(other[1], begun))
    last_up = moved(last[:cut], NEXT_UP, back=True)
    last_down = moved(last[cut:], NEXT_DOWN, back=True)
    first = from_core(tied(other[2], begun))
    steps.begin(begun)
    steps.go(1)
    along = core == 0
    zero = jnp.zeros((), bf16)
    to_up = jnp.where(along, widened(last_up, 2 * cut, 0), zero)
    to_down = jnp.where(along, widened(last_down, 2 * cut, cut), zero)
    next_up = total(mine[1][: 2 * cut], middle[: 2 * cut], to_up)
    next_down = total(mine[1][2 * cut :], middle[2 * cut :], to_down)
    next_up = moved(tied(next_up, steps.x), NEXT_UP, back=True)
    next_down = moved(next_down, NEXT_DOWN, back=True)
    far = [jnp.where(along, zero, x[:own]) for x in (last_up, last_down)]
    far = total(mine[2][:own], first[:own], *far)
    half_up = moved(far[:half], HALF_UP, back=True)
    half_down = moved(far[half:], HALF_DOWN, back=True)
    steps.go(2)
    steps.after(half_up[:1, :8], half_down[:1, :8])
    steps.go(2)

    def near(k):
        at = slice(k * own, (k + 1) * own)
        return [mine[2][own:][at], first[own:][at], next_up[at], next_down[at]]

    up = tied(total(*near(1), widened(half_up, own, 0)), steps.x)
    down = total(*near(2), widened(half_down, own, half))
    ends = moved(up, FIRST_UP, back=True), moved(down, FIRST_DOWN, back=True)
    return total(*near(0), *ends)


def local(features, weight, tile_values, tile_cols, tile_live, cotangent):
    n_rows, n_rep = lax.axis_size("rows"), lax.axis_size("rep")
    rep = lax.axis_index("rep")
    node_dev, width = features.shape
    tile = tile_values.shape[2]
    own = node_dev // tile
    group_tiles = own * n_rep
    core = rep % 2
    plans = [layout(own, c) for c in range(2)]
    groups = [len(keys) for keys in plans[0]]
    table = np.zeros((2, 3, n_rep // 2, own), np.int32)
    for c, plan in enumerate(plans):
        for at, key in enumerate(sum(plan, [])):
            if key:
                table[(c, *key)] = at
    place = jnp.mod(tile_cols // group_tiles - lax.axis_index("rows") + 1, n_rows)
    inner = tile_cols % group_tiles
    owner = inner // own
    dy = jnp.mod(owner // 2 - rep // 2, n_rep // 2)
    key = (((owner % 2) * 3 + place) * (n_rep // 2) + dy) * own + inner % own
    hit = key[:, :, None] == jnp.arange(table.size, dtype=jnp.int32)
    at = jnp.sum(jnp.where(hit, jnp.asarray(table.reshape(-1)), 0), axis=2)
    idx = jnp.mod(owner + rep, 2) * sum(groups) + at
    cnt = jnp.sum(tile_live, axis=1)

    parts = gather(features, core)
    output, term, *grads = layer(idx, cnt, tile_values, parts, weight, cotangent, groups)
    steps = Steps(term, core)
    grad = scatter(grads[: len(groups)], grads[len(groups) :], own, core, steps)
    weight_grad = steps.whole()
    feature_grad = jnp.swapaxes(grad, 1, 2).reshape(node_dev, width)
    return (output, feature_grad, weight_grad)


def solution(mesh):
    placed = (
        P(("rows", "rep"), None),
        P(),
        P(("rows", "rep"), None, None, None),
        P(("rows", "rep"), None),
        P(("rows", "rep"), None),
        P(("rows", "rep"), None),
    )
    return jax.shard_map(
        local,
        mesh=mesh,
        in_specs=placed,
        out_specs=(P(("rows", "rep"), None), P(("rows", "rep"), None), P()),
        check_vma=False,
    )
```

```python
import functools

import jax
import jax.numpy as jnp
import numpy as np
from jax import lax
from jax.experimental import pallas as pl
from jax.experimental.pallas import tpu as pltpu
from jax.sharding import PartitionSpec as P

bf16, f32 = jnp.bfloat16, jnp.float32

FWD_SLOTS = 48
BWD_SLOTS = 24
STAGES = 8
CHUNK = 8


def layout(own, core):
    half = own // 2

    def shards(*keys):
        return [(p, dy, i) for p, dy in keys for i in range(own)]

    if core == 0:
        last = shards((1, 2), (0, 2), (2, 2))
        middle = shards((1, 1), (0, 1), (2, 1), (1, 3), (0, 3), (2, 3))
        first = [None] * own + shards((1, 0), (0, 0), (2, 0))
    else:
        last = shards((0, 2)) + [None] * half + shards((2, 2)) + [None] * half
        middle = shards((0, 0), (0, 1), (0, 3), (2, 0), (2, 1), (2, 3))
        first = shards((1, 2), (1, 0), (1, 1), (1, 3))
    return last, middle, first


def kernel(n_in, n_out, idx, cnt, values, *refs):
    parts = refs[:n_in]
    w_ref, cot_ref, out_ref, wg_ref = refs[n_in : n_in + 4]
    outs = refs[n_in + 4 : n_in + 4 + n_out]
    a_ref, win, acc, stage, in_sem, a_sem, out_sem = refs[n_in + 4 + n_out :]
    n_tiles, _, tile, _ = a_ref.shape
    width = w_ref.shape[0]
    copies, row = [], 0
    for k, part in enumerate(parts):
        rows = part.shape[0]
        copies.append(pltpu.make_async_copy(part, win.at[pl.ds(row, rows)], in_sem.at[k]))
        row += rows
    blocks = [pltpu.make_async_copy(values.at[t], a_ref.at[t], a_sem.at[t]) for t in range(n_tiles)]
    for copy in copies + blocks:
        copy.start()
    wg_ref[...] = jnp.zeros_like(wg_ref)

    def zero(i, _):
        acc[pl.ds(i * 8, 8)] = jnp.zeros((8,) + acc.shape[1:], f32)
        return 0

    lax.fori_loop(0, acc.shape[0] // 8, zero, 0)
    for copy in copies:
        copy.wait()

    def row_tile(t, _):
        pltpu.make_async_copy(values.at[t], a_ref.at[t], a_sem.at[t]).wait()
        n = cnt[t]

        def lanes(k0, count):
            got = []
            for j in range(count):
                a = a_ref[t, k0 + j]
                got.append(jnp.where(k0 + j < n, a, jnp.zeros_like(a)))
            return jnp.concatenate(got, axis=1)

        def forward(i, af):
            k0 = i * FWD_SLOTS
            rows = [
                win[pl.ds(pl.multiple_of(idx[t, k0 + j] * tile, tile), tile), :]
                for j in range(FWD_SLOTS)
            ]
            return af + jnp.dot(
                lanes(k0, FWD_SLOTS), jnp.concatenate(rows, axis=0), preferred_element_type=f32
            )

        at = pl.ds(pl.multiple_of(t * tile, tile), tile)
        trips = (n + FWD_SLOTS - 1) // FWD_SLOTS
        af = lax.fori_loop(0, trips, forward, jnp.zeros((tile, width), f32)).astype(bf16)
        pre = jnp.dot(af, w_ref[...], preferred_element_type=f32)
        sig = jax.nn.sigmoid(pre)
        out_ref[at, :] = (pre * sig).astype(bf16)
        g = (cot_ref[at, :].astype(f32) * sig * (1.0 + pre * (1.0 - sig))).astype(bf16)
        wg_ref[...] += lax.dot_general(
            af, g, (((0,), (0,)), ((), ())), preferred_element_type=f32
        )
        gwt = lax.dot_general(
            w_ref[...], g, (((1,), (1,)), ((), ())), preferred_element_type=f32
        ).astype(bf16)

        def backward(i, _):
            k0 = i * BWD_SLOTS
            r = jnp.dot(gwt, lanes(k0, BWD_SLOTS), preferred_element_type=f32)
            for j in range(BWD_SLOTS):
                acc[idx[t, k0 + j]] += r[:, j * tile : (j + 1) * tile]
            return 0

        lax.fori_loop(0, (n + BWD_SLOTS - 1) // BWD_SLOTS, backward, 0)
        return 0

    lax.fori_loop(0, n_tiles, row_tile, 0)
    stages, chunk = stage.shape[:2]

    def copy(slot, out, at):
        return pltpu.make_async_copy(stage.at[slot], out.at[pl.ds(at, chunk)], out_sem.at[slot])

    done = 0
    for out in outs:
        steps = out.shape[0] // chunk

        def emit(i, _, out=out, done=done):
            number = done + i
            slot = lax.rem(number, stages)

            @pl.when(number >= stages)
            def _():
                copy(slot, out, 0).wait()

            stage[slot] = acc[pl.ds(number * chunk, chunk)].astype(bf16)
            copy(slot, out, i * chunk).start()
            return 0

        lax.fori_loop(0, steps, emit, 0)
        done += steps
    for slot in range(stages):
        copy(slot, outs[0], 0).wait()


def layer(idx, cnt, tile_values, parts, weight, cotangent, groups):
    nt, _, tile, _ = tile_values.shape
    width = weight.shape[0]
    n_win = 2 * sum(groups)
    smem = pl.BlockSpec(memory_space=pltpu.SMEM)
    vmem = pl.BlockSpec(memory_space=pltpu.VMEM)
    anywhere = pl.BlockSpec(memory_space=pl.ANY)
    return pl.pallas_call(
        functools.partial(kernel, len(parts), 2 * len(groups)),
        in_specs=[smem, smem] + [anywhere] * (1 + len(parts)) + [vmem, vmem],
        out_specs=[vmem, vmem] + [anywhere] * (2 * len(groups)),
        scratch_shapes=[
            pltpu.VMEM(tile_values.shape, bf16),
            pltpu.VMEM((n_win * tile, width), bf16),
            pltpu.VMEM((n_win, width, tile), f32),
            pltpu.VMEM((STAGES, CHUNK, width, tile), bf16),
            pltpu.SemaphoreType.DMA((len(parts),)),
            pltpu.SemaphoreType.DMA((nt,)),
            pltpu.SemaphoreType.DMA((STAGES,)),
        ],
        out_shape=[
            jax.ShapeDtypeStruct((nt * tile, width), bf16),
            jax.ShapeDtypeStruct((width, width), f32),
        ]
        + [jax.ShapeDtypeStruct((g, width, tile), bf16) for _ in range(2) for g in groups],
        compiler_params=pltpu.CompilerParams(vmem_limit_bytes=60 * 2**20),
        cost_estimate=pl.CostEstimate(
            flops=4 * tile_values.size * width,
            bytes_accessed=6 * tile_values.size,
            transcendentals=0,
        ),
    )(idx, cnt, tile_values, *parts, weight, cotangent)


def tied(x, *earlier):
    return pl.pallas_call(
        lambda *refs: None,
        in_specs=[pl.BlockSpec(memory_space=pl.ANY)] * (1 + len(earlier)),
        out_specs=pl.BlockSpec(memory_space=pl.ANY),
        out_shape=jax.ShapeDtypeStruct(x.shape, x.dtype),
        input_output_aliases={0: 0},
    )(x, *earlier)


def near(group, rep, axis, step, n_rows, n_rep):
    if axis == "z":
        return (group + step) % n_rows * n_rep + rep
    return group * n_rep + (rep + 2 * step) % n_rep


def moved(x, moves, back=False):
    n_rows, n_rep = lax.axis_size("rows"), lax.axis_size("rep")
    pairs = []
    for group in range(n_rows):
        for rep in range(n_rep):
            if moves[rep % 2]:
                source = near(group, rep, *moves[rep % 2], n_rows, n_rep)
                pairs.append((source, group * n_rep + rep))
    if back:
        pairs = [(target, source) for source, target in pairs]
    return lax.ppermute(x, ("rows", "rep"), pairs)


FIRST_UP, FIRST_DOWN = (("z", -1), ("y", 1)), (("z", 1), ("y", -1))
HALF_UP, HALF_DOWN = (None, ("y", 1)), (None, ("y", -1))
NEXT_UP, NEXT_DOWN = (("y", 1), ("z", -1)), (("y", -1), ("z", 1))


def from_core(x):
    return lax.ppermute(x, "rep", [(i, i ^ 1) for i in range(lax.axis_size("rep"))])


def gather(features, core):
    rows = features.shape[0]
    half = rows // 2
    up, down = moved(features, FIRST_UP), moved(features, FIRST_DOWN)
    near3 = jnp.concatenate([features, up, down])
    far = jnp.concatenate([moved(up[:half], HALF_UP), moved(down[half:], HALF_DOWN)])
    up, down = moved(near3, NEXT_UP), moved(near3, NEXT_DOWN)
    crossing = jnp.concatenate([far, far[:half]])
    swapped = from_core(near3)
    swapped_far = from_core(far)
    to_up = jnp.where(core == 0, up[: 3 * half], crossing)
    to_down = jnp.where(core == 0, down[3 * half :], crossing)
    last_up = moved(tied(to_up, swapped[:8], swapped_far[:8]), NEXT_UP)
    last_down = moved(to_down, NEXT_DOWN)
    mine = [last_up, last_down, up, down]
    return mine + [far, near3] + [from_core(x) for x in mine] + [swapped_far, swapped]


class Steps:
    def __init__(self, term, core):
        height = term.shape[0] // 2
        low, high = term[:height], term[height:]
        self.mine = jnp.where(core == 0, low, high)
        self.got = from_core(jnp.where(core == 0, high, low))
        self.core = core
        self.left = [
            (axis, bit)
            for axis, first in (("rep", 2), ("rows", 1))
            for bit in (1 << k for k in range(10))
            if first <= bit < lax.axis_size(axis)
        ]

    def begin(self, *earlier):
        self.x = self.mine + tied(self.got, *earlier)

    def go(self, count):
        for axis, bit in self.left[:count]:
            pairs = [(i, i ^ bit) for i in range(lax.axis_size(axis))]
            rounded = lax.reduce_precision(self.x, 8, 7)
            self.x = rounded + lax.ppermute(rounded.astype(bf16), axis, pairs).astype(f32)
        self.left = self.left[count:]

    def after(self, *earlier):
        self.x = tied(self.x, *earlier)

    def whole(self):
        self.go(len(self.left))
        other = from_core(self.x)
        halves = [self.x, other], [other, self.x]
        return jnp.where(self.core == 0, *(jnp.concatenate(h) for h in halves))


def total(*terms):
    return sum(x.astype(f32) for x in terms).astype(bf16)


def widened(x, size, at):
    return jnp.pad(x, ((at, size - at - x.shape[0]), (0, 0), (0, 0)))


def scatter(mine, other, own, core, steps):
    half = own // 2
    cut = 3 * half
    last = total(mine[0], from_core(other[0]))
    begun = last[:1, :8]
    middle = from_core(tied(other[1], begun))
    last_up = moved(last[:cut], NEXT_UP, back=True)
    last_down = moved(last[cut:], NEXT_DOWN, back=True)
    first = from_core(tied(other[2], begun))
    steps.begin(begun)
    steps.go(1)
    along = core == 0
    zero = jnp.zeros((), bf16)
    to_up = jnp.where(along, widened(last_up, 2 * cut, 0), zero)
    to_down = jnp.where(along, widened(last_down, 2 * cut, cut), zero)
    next_up = total(mine[1][: 2 * cut], middle[: 2 * cut], to_up)
    next_down = total(mine[1][2 * cut :], middle[2 * cut :], to_down)
    next_up = moved(tied(next_up, steps.x), NEXT_UP, back=True)
    next_down = moved(next_down, NEXT_DOWN, back=True)
    far = [jnp.where(along, zero, x[:own]) for x in (last_up, last_down)]
    far = total(mine[2][:own], first[:own], *far)
    half_up = moved(far[:half], HALF_UP, back=True)
    half_down = moved(far[half:], HALF_DOWN, back=True)
    steps.go(1)
    steps.after(half_up[:1, :8], half_down[:1, :8])
    steps.go(2)

    def near(k):
        at = slice(k * own, (k + 1) * own)
        return [mine[2][own:][at], first[own:][at], next_up[at], next_down[at]]

    up = tied(total(*near(1), widened(half_up, own, 0)), steps.x)
    down = total(*near(2), widened(half_down, own, half))
    ends = moved(up, FIRST_UP, back=True), moved(down, FIRST_DOWN, back=True)
    steps.after(down[:1, :8])
    steps.go(2)
    steps.after(ends[0][:1, :8])
    return total(*near(0), *ends)


def local(features, weight, tile_values, tile_cols, tile_live, cotangent):
    n_rows, n_rep = lax.axis_size("rows"), lax.axis_size("rep")
    rep = lax.axis_index("rep")
    node_dev, width = features.shape
    tile = tile_values.shape[2]
    own = node_dev // tile
    group_tiles = own * n_rep
    core = rep % 2
    plans = [layout(own, c) for c in range(2)]
    groups = [len(keys) for keys in plans[0]]
    table = np.zeros((2, 3, n_rep // 2, own), np.int32)
    for c, plan in enumerate(plans):
        for at, key in enumerate(sum(plan, [])):
            if key:
                table[(c, *key)] = at
    place = jnp.mod(tile_cols // group_tiles - lax.axis_index("rows") + 1, n_rows)
    inner = tile_cols % group_tiles
    owner = inner // own
    dy = jnp.mod(owner // 2 - rep // 2, n_rep // 2)
    key = (((owner % 2) * 3 + place) * (n_rep // 2) + dy) * own + inner % own
    hit = key[:, :, None] == jnp.arange(table.size, dtype=jnp.int32)
    at = jnp.sum(jnp.where(hit, jnp.asarray(table.reshape(-1)), 0), axis=2)
    idx = jnp.mod(owner + rep, 2) * sum(groups) + at
    cnt = jnp.sum(tile_live, axis=1)

    parts = gather(features, core)
    output, term, *grads = layer(idx, cnt, tile_values, parts, weight, cotangent, groups)
    steps = Steps(term, core)
    grad = scatter(grads[: len(groups)], grads[len(groups) :], own, core, steps)
    weight_grad = steps.whole()
    feature_grad = jnp.swapaxes(grad, 1, 2).reshape(node_dev, width)
    return (output, feature_grad, weight_grad)


def solution(mesh):
    placed = (
        P(("rows", "rep"), None),
        P(),
        P(("rows", "rep"), None, None, None),
        P(("rows", "rep"), None),
        P(("rows", "rep"), None),
        P(("rows", "rep"), None),
    )
    return jax.shard_map(
        local,
        mesh=mesh,
        in_specs=placed,
        out_specs=(P(("rows", "rep"), None), P(("rows", "rep"), None), P()),
        check_vma=False,
    )
```

```python
import functools

import jax
import jax.numpy as jnp
import numpy as np
from jax import lax
from jax.experimental import pallas as pl
from jax.experimental.pallas import tpu as pltpu
from jax.sharding import PartitionSpec as P

bf16, f32 = jnp.bfloat16, jnp.float32

FWD_SLOTS = 48
BWD_SLOTS = 24
STAGES = 8
CHUNK = 8


def layout(own, core):
    half = own // 2

    def shards(*keys):
        return [(p, dy, i) for p, dy in keys for i in range(own)]

    if core == 0:
        last = shards((1, 2), (0, 2), (2, 2))
        middle = shards((1, 1), (0, 1), (2, 1), (1, 3), (0, 3), (2, 3))
        first = [None] * own + shards((1, 0), (0, 0), (2, 0))
    else:
        last = shards((0, 2)) + [None] * half + shards((2, 2)) + [None] * half
        middle = shards((0, 0), (0, 1), (0, 3), (2, 0), (2, 1), (2, 3))
        first = shards((1, 2), (1, 0), (1, 1), (1, 3))
    return last, middle, first


def kernel(n_in, n_out, idx, cnt, values, *refs):
    parts = refs[:n_in]
    w_ref, cot_ref, out_ref, wg_ref = refs[n_in : n_in + 4]
    outs = refs[n_in + 4 : n_in + 4 + n_out]
    a_ref, win, acc, stage, in_sem, a_sem, out_sem = refs[n_in + 4 + n_out :]
    n_tiles, _, tile, _ = a_ref.shape
    width = w_ref.shape[0]
    copies, row = [], 0
    for k, part in enumerate(parts):
        rows = part.shape[0]
        copies.append(pltpu.make_async_copy(part, win.at[pl.ds(row, rows)], in_sem.at[k]))
        row += rows
    blocks = [pltpu.make_async_copy(values.at[t], a_ref.at[t], a_sem.at[t]) for t in range(n_tiles)]
    for copy in copies + blocks:
        copy.start()
    wg_ref[...] = jnp.zeros_like(wg_ref)

    def zero(i, _):
        acc[pl.ds(i * 8, 8)] = jnp.zeros((8,) + acc.shape[1:], f32)
        return 0

    lax.fori_loop(0, acc.shape[0] // 8, zero, 0)
    for copy in copies:
        copy.wait()

    def row_tile(t, _):
        pltpu.make_async_copy(values.at[t], a_ref.at[t], a_sem.at[t]).wait()
        n = cnt[t]

        def lanes(k0, count):
            got = []
            for j in range(count):
                a = a_ref[t, k0 + j]
                got.append(jnp.where(k0 + j < n, a, jnp.zeros_like(a)))
            return jnp.concatenate(got, axis=1)

        def forward(i, af):
            k0 = i * FWD_SLOTS
            rows = [
                win[pl.ds(pl.multiple_of(idx[t, k0 + j] * tile, tile), tile), :]
                for j in range(FWD_SLOTS)
            ]
            return af + jnp.dot(
                lanes(k0, FWD_SLOTS), jnp.concatenate(rows, axis=0), preferred_element_type=f32
            )

        at = pl.ds(pl.multiple_of(t * tile, tile), tile)
        trips = (n + FWD_SLOTS - 1) // FWD_SLOTS
        af = lax.fori_loop(0, trips, forward, jnp.zeros((tile, width), f32)).astype(bf16)
        pre = jnp.dot(af, w_ref[...], preferred_element_type=f32)
        sig = jax.nn.sigmoid(pre)
        out_ref[at, :] = (pre * sig).astype(bf16)
        g = (cot_ref[at, :].astype(f32) * sig * (1.0 + pre * (1.0 - sig))).astype(bf16)
        wg_ref[...] += lax.dot_general(
            af, g, (((0,), (0,)), ((), ())), preferred_element_type=f32
        )
        gwt = lax.dot_general(
            w_ref[...], g, (((1,), (1,)), ((), ())), preferred_element_type=f32
        ).astype(bf16)

        def backward(i, _):
            k0 = i * BWD_SLOTS
            r = jnp.dot(gwt, lanes(k0, BWD_SLOTS), preferred_element_type=f32)
            for j in range(BWD_SLOTS):
                acc[idx[t, k0 + j]] += r[:, j * tile : (j + 1) * tile]
            return 0

        lax.fori_loop(0, (n + BWD_SLOTS - 1) // BWD_SLOTS, backward, 0)
        return 0

    lax.fori_loop(0, n_tiles, row_tile, 0)
    stages, chunk = stage.shape[:2]

    def copy(slot, out, at):
        return pltpu.make_async_copy(stage.at[slot], out.at[pl.ds(at, chunk)], out_sem.at[slot])

    done = 0
    for out in outs:
        steps = out.shape[0] // chunk

        def emit(i, _, out=out, done=done):
            number = done + i
            slot = lax.rem(number, stages)

            @pl.when(number >= stages)
            def _():
                copy(slot, out, 0).wait()

            stage[slot] = acc[pl.ds(number * chunk, chunk)].astype(bf16)
            copy(slot, out, i * chunk).start()
            return 0

        lax.fori_loop(0, steps, emit, 0)
        done += steps
    for slot in range(stages):
        copy(slot, outs[0], 0).wait()


def layer(idx, cnt, tile_values, parts, weight, cotangent, groups):
    nt, _, tile, _ = tile_values.shape
    width = weight.shape[0]
    n_win = 2 * sum(groups)
    smem = pl.BlockSpec(memory_space=pltpu.SMEM)
    vmem = pl.BlockSpec(memory_space=pltpu.VMEM)
    anywhere = pl.BlockSpec(memory_space=pl.ANY)
    return pl.pallas_call(
        functools.partial(kernel, len(parts), 2 * len(groups)),
        in_specs=[smem, smem] + [anywhere] * (1 + len(parts)) + [vmem, vmem],
        out_specs=[vmem, vmem] + [anywhere] * (2 * len(groups)),
        scratch_shapes=[
            pltpu.VMEM(tile_values.shape, bf16),
            pltpu.VMEM((n_win * tile, width), bf16),
            pltpu.VMEM((n_win, width, tile), f32),
            pltpu.VMEM((STAGES, CHUNK, width, tile), bf16),
            pltpu.SemaphoreType.DMA((len(parts),)),
            pltpu.SemaphoreType.DMA((nt,)),
            pltpu.SemaphoreType.DMA((STAGES,)),
        ],
        out_shape=[
            jax.ShapeDtypeStruct((nt * tile, width), bf16),
            jax.ShapeDtypeStruct((width, width), f32),
        ]
        + [jax.ShapeDtypeStruct((g, width, tile), bf16) for _ in range(2) for g in groups],
        compiler_params=pltpu.CompilerParams(vmem_limit_bytes=60 * 2**20),
        cost_estimate=pl.CostEstimate(
            flops=4 * tile_values.size * width,
            bytes_accessed=6 * tile_values.size,
            transcendentals=0,
        ),
    )(idx, cnt, tile_values, *parts, weight, cotangent)


def tied(x, *earlier):
    return pl.pallas_call(
        lambda *refs: None,
        in_specs=[pl.BlockSpec(memory_space=pl.ANY)] * (1 + len(earlier)),
        out_specs=pl.BlockSpec(memory_space=pl.ANY),
        out_shape=jax.ShapeDtypeStruct(x.shape, x.dtype),
        input_output_aliases={0: 0},
    )(x, *earlier)


def near(group, rep, axis, step, n_rows, n_rep):
    if axis == "z":
        return (group + step) % n_rows * n_rep + rep
    return group * n_rep + (rep + 2 * step) % n_rep


def moved(x, moves, back=False):
    n_rows, n_rep = lax.axis_size("rows"), lax.axis_size("rep")
    pairs = []
    for group in range(n_rows):
        for rep in range(n_rep):
            if moves[rep % 2]:
                source = near(group, rep, *moves[rep % 2], n_rows, n_rep)
                pairs.append((source, group * n_rep + rep))
    if back:
        pairs = [(target, source) for source, target in pairs]
    return lax.ppermute(x, ("rows", "rep"), pairs)


FIRST_UP, FIRST_DOWN = (("z", -1), ("y", 1)), (("z", 1), ("y", -1))
HALF_UP, HALF_DOWN = (None, ("y", 1)), (None, ("y", -1))
NEXT_UP, NEXT_DOWN = (("y", 1), ("z", -1)), (("y", -1), ("z", 1))


def from_core(x):
    return lax.ppermute(x, "rep", [(i, i ^ 1) for i in range(lax.axis_size("rep"))])


def gather(features, core):
    rows = features.shape[0]
    half = rows // 2
    up, down = moved(features, FIRST_UP), moved(features, FIRST_DOWN)
    near3 = jnp.concatenate([features, up, down])
    far = jnp.concatenate([moved(up[:half], HALF_UP), moved(down[half:], HALF_DOWN)])
    up, down = moved(near3, NEXT_UP), moved(near3, NEXT_DOWN)
    crossing = jnp.concatenate([far, far[:half]])
    swapped = from_core(near3)
    swapped_far = from_core(far)
    to_up = jnp.where(core == 0, up[: 3 * half], crossing)
    to_down = jnp.where(core == 0, down[3 * half :], crossing)
    last_up = moved(tied(to_up, swapped[:8], swapped_far[:8]), NEXT_UP)
    last_down = moved(to_down, NEXT_DOWN)
    mine = [last_up, last_down, up, down]
    return mine + [far, near3] + [from_core(x) for x in mine] + [swapped_far, swapped]


class Steps:
    def __init__(self, term, core):
        height = term.shape[0] // 2
        low, high = term[:height], term[height:]
        self.mine = jnp.where(core == 0, low, high)
        self.got = from_core(jnp.where(core == 0, high, low))
        self.core = core
        self.left = [("rep", (2,)), ("rep", (4,)), ("rows", (1, 2)), ("rows", (4, 8))]

    def begin(self, *earlier):
        self.x = self.mine + tied(self.got, *earlier)

    def go(self, count):
        for axis, bits in self.left[:count]:
            own = lax.reduce_precision(self.x, 8, 7)
            sent = own.astype(bf16)

            def taken(bit, axis=axis, sent=sent):
                pairs = [(i, i ^ bit) for i in range(lax.axis_size(axis))]
                return lax.ppermute(sent, axis, pairs).astype(f32)

            self.x = own + taken(bits[0])
            if len(bits) > 1:
                self.x += taken(bits[1]) + taken(bits[0] | bits[1])
        self.left = self.left[count:]

    def after(self, *earlier):
        self.x = tied(self.x, *earlier)

    def whole(self):
        self.go(len(self.left))
        other = from_core(self.x)
        halves = [self.x, other], [other, self.x]
        return jnp.where(self.core == 0, *(jnp.concatenate(h) for h in halves))


def total(*terms):
    return sum(x.astype(f32) for x in terms).astype(bf16)


def widened(x, size, at):
    return jnp.pad(x, ((at, size - at - x.shape[0]), (0, 0), (0, 0)))


def scatter(mine, other, own, core, steps):
    half = own // 2
    cut = 3 * half
    last = total(mine[0], from_core(other[0]))
    begun = last[:1, :8]
    middle = from_core(tied(other[1], begun))
    last_up = moved(last[:cut], NEXT_UP, back=True)
    last_down = moved(last[cut:], NEXT_DOWN, back=True)
    first = from_core(tied(other[2], begun))
    steps.begin(begun)
    steps.go(1)
    along = core == 0
    zero = jnp.zeros((), bf16)
    to_up = jnp.where(along, widened(last_up, 2 * cut, 0), zero)
    to_down = jnp.where(along, widened(last_down, 2 * cut, cut), zero)
    next_up = total(mine[1][: 2 * cut], middle[: 2 * cut], to_up)
    next_down = total(mine[1][2 * cut :], middle[2 * cut :], to_down)
    next_up = moved(tied(next_up, steps.x), NEXT_UP, back=True)
    next_down = moved(next_down, NEXT_DOWN, back=True)
    far = [jnp.where(along, zero, x[:own]) for x in (last_up, last_down)]
    far = total(mine[2][:own], first[:own], *far)
    half_up = moved(far[:half], HALF_UP, back=True)
    half_down = moved(far[half:], HALF_DOWN, back=True)
    steps.go(1)
    steps.after(half_up[:1, :8], half_down[:1, :8])
    steps.go(2)

    def near(k):
        at = slice(k * own, (k + 1) * own)
        return [mine[2][own:][at], first[own:][at], next_up[at], next_down[at]]

    up = tied(total(*near(1), widened(half_up, own, 0)), steps.x)
    down = total(*near(2), widened(half_down, own, half))
    ends = moved(up, FIRST_UP, back=True), moved(down, FIRST_DOWN, back=True)
    return total(*near(0), *ends)


def local(features, weight, tile_values, tile_cols, tile_live, cotangent):
    n_rows, n_rep = lax.axis_size("rows"), lax.axis_size("rep")
    rep = lax.axis_index("rep")
    node_dev, width = features.shape
    tile = tile_values.shape[2]
    own = node_dev // tile
    group_tiles = own * n_rep
    core = rep % 2
    plans = [layout(own, c) for c in range(2)]
    groups = [len(keys) for keys in plans[0]]
    table = np.zeros((2, 3, n_rep // 2, own), np.int32)
    for c, plan in enumerate(plans):
        for at, key in enumerate(sum(plan, [])):
            if key:
                table[(c, *key)] = at
    place = jnp.mod(tile_cols // group_tiles - lax.axis_index("rows") + 1, n_rows)
    inner = tile_cols % group_tiles
    owner = inner // own
    dy = jnp.mod(owner // 2 - rep // 2, n_rep // 2)
    key = (((owner % 2) * 3 + place) * (n_rep // 2) + dy) * own + inner % own
    hit = key[:, :, None] == jnp.arange(table.size, dtype=jnp.int32)
    at = jnp.sum(jnp.where(hit, jnp.asarray(table.reshape(-1)), 0), axis=2)
    idx = jnp.mod(owner + rep, 2) * sum(groups) + at
    cnt = jnp.sum(tile_live, axis=1)

    parts = gather(features, core)
    output, term, *grads = layer(idx, cnt, tile_values, parts, weight, cotangent, groups)
    steps = Steps(term, core)
    grad = scatter(grads[: len(groups)], grads[len(groups) :], own, core, steps)
    weight_grad = steps.whole()
    feature_grad = jnp.swapaxes(grad, 1, 2).reshape(node_dev, width)
    return (output, feature_grad, weight_grad)


def solution(mesh):
    placed = (
        P(("rows", "rep"), None),
        P(),
        P(("rows", "rep"), None, None, None),
        P(("rows", "rep"), None),
        P(("rows", "rep"), None),
        P(("rows", "rep"), None),
    )
    return jax.shard_map(
        local,
        mesh=mesh,
        in_specs=placed,
        out_specs=(P(("rows", "rep"), None), P(("rows", "rep"), None), P()),
        check_vma=False,
    )
```

```python
import functools

import jax
import jax.numpy as jnp
import numpy as np
from jax import lax
from jax.experimental import pallas as pl
from jax.experimental.pallas import tpu as pltpu
from jax.sharding import PartitionSpec as P

bf16, f32 = jnp.bfloat16, jnp.float32

FWD_SLOTS = 48
BWD_SLOTS = 24
STAGES = 8
CHUNK = 8


def layout(own, core):
    half = own // 2

    def shards(*keys):
        return [(p, dy, i) for p, dy in keys for i in range(own)]

    if core == 0:
        last = shards((1, 2), (0, 2), (2, 2))
        middle = shards((1, 1), (0, 1), (2, 1), (1, 3), (0, 3), (2, 3))
        first = [None] * own + shards((1, 0), (0, 0), (2, 0))
    else:
        last = shards((0, 2)) + [None] * half + shards((2, 2)) + [None] * half
        middle = shards((0, 0), (0, 1), (0, 3), (2, 0), (2, 1), (2, 3))
        first = shards((1, 2), (1, 0), (1, 1), (1, 3))
    return last, middle, first


def kernel(n_in, n_out, idx, cnt, values, *refs):
    parts = refs[:n_in]
    w_ref, cot_ref, out_ref, wg_ref = refs[n_in : n_in + 4]
    outs = refs[n_in + 4 : n_in + 4 + n_out]
    a_ref, win, acc, stage, in_sem, a_sem, out_sem = refs[n_in + 4 + n_out :]
    n_tiles, _, tile, _ = a_ref.shape
    width = w_ref.shape[0]
    copies, row = [], 0
    for k, part in enumerate(parts):
        rows = part.shape[0]
        copies.append(pltpu.make_async_copy(part, win.at[pl.ds(row, rows)], in_sem.at[k]))
        row += rows
    blocks = [pltpu.make_async_copy(values.at[t], a_ref.at[t], a_sem.at[t]) for t in range(n_tiles)]
    for copy in copies + blocks:
        copy.start()
    wg_ref[...] = jnp.zeros_like(wg_ref)

    def zero(i, _):
        acc[pl.ds(i * 8, 8)] = jnp.zeros((8,) + acc.shape[1:], f32)
        return 0

    lax.fori_loop(0, acc.shape[0] // 8, zero, 0)
    for copy in copies:
        copy.wait()

    def row_tile(t, _):
        pltpu.make_async_copy(values.at[t], a_ref.at[t], a_sem.at[t]).wait()
        n = cnt[t]

        def lanes(k0, count):
            got = []
            for j in range(count):
                a = a_ref[t, k0 + j]
                got.append(jnp.where(k0 + j < n, a, jnp.zeros_like(a)))
            return jnp.concatenate(got, axis=1)

        def forward(i, af):
            k0 = i * FWD_SLOTS
            rows = [
                win[pl.ds(pl.multiple_of(idx[t, k0 + j] * tile, tile), tile), :]
                for j in range(FWD_SLOTS)
            ]
            return af + jnp.dot(
                lanes(k0, FWD_SLOTS), jnp.concatenate(rows, axis=0), preferred_element_type=f32
            )

        at = pl.ds(pl.multiple_of(t * tile, tile), tile)
        trips = (n + FWD_SLOTS - 1) // FWD_SLOTS
        af = lax.fori_loop(0, trips, forward, jnp.zeros((tile, width), f32)).astype(bf16)
        pre = jnp.dot(af, w_ref[...], preferred_element_type=f32)
        sig = jax.nn.sigmoid(pre)
        out_ref[at, :] = (pre * sig).astype(bf16)
        g = (cot_ref[at, :].astype(f32) * sig * (1.0 + pre * (1.0 - sig))).astype(bf16)
        wg_ref[...] += lax.dot_general(
            af, g, (((0,), (0,)), ((), ())), preferred_element_type=f32
        )
        gwt = lax.dot_general(
            w_ref[...], g, (((1,), (1,)), ((), ())), preferred_element_type=f32
        ).astype(bf16)

        def backward(i, _):
            k0 = i * BWD_SLOTS
            r = jnp.dot(gwt, lanes(k0, BWD_SLOTS), preferred_element_type=f32)
            for j in range(BWD_SLOTS):
                acc[idx[t, k0 + j]] += r[:, j * tile : (j + 1) * tile]
            return 0

        lax.fori_loop(0, (n + BWD_SLOTS - 1) // BWD_SLOTS, backward, 0)
        return 0

    lax.fori_loop(0, n_tiles, row_tile, 0)
    stages, chunk = stage.shape[:2]

    def copy(slot, out, at):
        return pltpu.make_async_copy(stage.at[slot], out.at[pl.ds(at, chunk)], out_sem.at[slot])

    done = 0
    for out in outs:
        steps = out.shape[0] // chunk

        def emit(i, _, out=out, done=done):
            number = done + i
            slot = lax.rem(number, stages)

            @pl.when(number >= stages)
            def _():
                copy(slot, out, 0).wait()

            stage[slot] = acc[pl.ds(number * chunk, chunk)].astype(bf16)
            copy(slot, out, i * chunk).start()
            return 0

        lax.fori_loop(0, steps, emit, 0)
        done += steps
    for slot in range(stages):
        copy(slot, outs[0], 0).wait()


def layer(idx, cnt, tile_values, parts, weight, cotangent, groups):
    nt, _, tile, _ = tile_values.shape
    width = weight.shape[0]
    n_win = 2 * sum(groups)
    smem = pl.BlockSpec(memory_space=pltpu.SMEM)
    vmem = pl.BlockSpec(memory_space=pltpu.VMEM)
    anywhere = pl.BlockSpec(memory_space=pl.ANY)
    return pl.pallas_call(
        functools.partial(kernel, len(parts), 2 * len(groups)),
        in_specs=[smem, smem] + [anywhere] * (1 + len(parts)) + [vmem, vmem],
        out_specs=[vmem, vmem] + [anywhere] * (2 * len(groups)),
        scratch_shapes=[
            pltpu.VMEM(tile_values.shape, bf16),
            pltpu.VMEM((n_win * tile, width), bf16),
            pltpu.VMEM((n_win, width, tile), f32),
            pltpu.VMEM((STAGES, CHUNK, width, tile), bf16),
            pltpu.SemaphoreType.DMA((len(parts),)),
            pltpu.SemaphoreType.DMA((nt,)),
            pltpu.SemaphoreType.DMA((STAGES,)),
        ],
        out_shape=[
            jax.ShapeDtypeStruct((nt * tile, width), bf16),
            jax.ShapeDtypeStruct((width, width), f32),
        ]
        + [jax.ShapeDtypeStruct((g, width, tile), bf16) for _ in range(2) for g in groups],
        compiler_params=pltpu.CompilerParams(vmem_limit_bytes=60 * 2**20),
        cost_estimate=pl.CostEstimate(
            flops=4 * tile_values.size * width,
            bytes_accessed=6 * tile_values.size,
            transcendentals=0,
        ),
    )(idx, cnt, tile_values, *parts, weight, cotangent)


def tied(x, *earlier):
    return pl.pallas_call(
        lambda *refs: None,
        in_specs=[pl.BlockSpec(memory_space=pl.ANY)] * (1 + len(earlier)),
        out_specs=pl.BlockSpec(memory_space=pl.ANY),
        out_shape=jax.ShapeDtypeStruct(x.shape, x.dtype),
        input_output_aliases={0: 0},
    )(x, *earlier)


def near(group, rep, axis, step, n_rows, n_rep):
    if axis == "z":
        return (group + step) % n_rows * n_rep + rep
    return group * n_rep + (rep + 2 * step) % n_rep


def moved(x, moves, back=False):
    n_rows, n_rep = lax.axis_size("rows"), lax.axis_size("rep")
    pairs = []
    for group in range(n_rows):
        for rep in range(n_rep):
            if moves[rep % 2]:
                source = near(group, rep, *moves[rep % 2], n_rows, n_rep)
                pairs.append((source, group * n_rep + rep))
    if back:
        pairs = [(target, source) for source, target in pairs]
    return lax.ppermute(x, ("rows", "rep"), pairs)


FIRST_UP, FIRST_DOWN = (("z", -1), ("y", 1)), (("z", 1), ("y", -1))
HALF_UP, HALF_DOWN = (None, ("y", 1)), (None, ("y", -1))
NEXT_UP, NEXT_DOWN = (("y", 1), ("z", -1)), (("y", -1), ("z", 1))


def from_core(x):
    return lax.ppermute(x, "rep", [(i, i ^ 1) for i in range(lax.axis_size("rep"))])


def gather(features, core):
    rows = features.shape[0]
    half = rows // 2
    up, down = moved(features, FIRST_UP), moved(features, FIRST_DOWN)
    near3 = jnp.concatenate([features, up, down])
    far = jnp.concatenate([moved(up[:half], HALF_UP), moved(down[half:], HALF_DOWN)])
    up, down = moved(near3, NEXT_UP), moved(near3, NEXT_DOWN)
    crossing = jnp.concatenate([far, far[:half]])
    swapped = from_core(near3)
    swapped_far = from_core(far)
    to_up = jnp.where(core == 0, up[: 3 * half], crossing)
    to_down = jnp.where(core == 0, down[3 * half :], crossing)
    last_up = moved(tied(to_up, swapped[:8], swapped_far[:8]), NEXT_UP)
    last_down = moved(to_down, NEXT_DOWN)
    mine = [last_up, last_down, up, down]
    return mine + [far, near3] + [from_core(x) for x in mine] + [swapped_far, swapped]


class Steps:
    def __init__(self, term, core):
        height = term.shape[0] // 2
        low, high = term[:height], term[height:]
        self.mine, self.other = jnp.where(core == 0, low, high), jnp.where(core == 0, high, low)
        self.core = core
        self.left = [
            (axis, bit)
            for axis, first in (("rep", 2), ("rows", 1))
            for bit in (1 << k for k in range(10))
            if first <= bit < lax.axis_size(axis)
        ]

    def begin(self, *earlier):
        self.x = self.mine + from_core(tied(self.other, *earlier))

    def go(self, count):
        for axis, bit in self.left[:count]:
            pairs = [(i, i ^ bit) for i in range(lax.axis_size(axis))]
            rounded = lax.reduce_precision(self.x, 8, 7)
            self.x = rounded + lax.ppermute(rounded.astype(bf16), axis, pairs).astype(f32)
        self.left = self.left[count:]

    def after(self, *earlier):
        self.x = tied(self.x, *earlier)

    def whole(self):
        self.go(len(self.left))
        other = from_core(self.x)
        halves = [self.x, other], [other, self.x]
        return jnp.where(self.core == 0, *(jnp.concatenate(h) for h in halves))


def total(*terms):
    return sum(x.astype(f32) for x in terms).astype(bf16)


def widened(x, size, at):
    return jnp.pad(x, ((at, size - at - x.shape[0]), (0, 0), (0, 0)))


def scatter(mine, other, own, core, steps):
    half = own // 2
    cut = 3 * half
    last = total(mine[0], from_core(other[0]))
    begun = last[:1, :8]
    middle = from_core(tied(other[1], begun))
    last_up = moved(last[:cut], NEXT_UP, back=True)
    last_down = moved(last[cut:], NEXT_DOWN, back=True)
    first = from_core(tied(other[2], begun))
    steps.begin(begun)
    steps.go(1)
    along = core == 0
    zero = jnp.zeros((), bf16)
    to_up = jnp.where(along, widened(last_up, 2 * cut, 0), zero)
    to_down = jnp.where(along, widened(last_down, 2 * cut, cut), zero)
    next_up = total(mine[1][: 2 * cut], middle[: 2 * cut], to_up)
    next_down = total(mine[1][2 * cut :], middle[2 * cut :], to_down)
    next_up = moved(tied(next_up, steps.x), NEXT_UP, back=True)
    next_down = moved(next_down, NEXT_DOWN, back=True)
    far = [jnp.where(along, zero, x[:own]) for x in (last_up, last_down)]
    far = total(mine[2][:own], first[:own], *far)
    half_up = moved(far[:half], HALF_UP, back=True)
    half_down = moved(far[half:], HALF_DOWN, back=True)
    steps.go(1)
    steps.after(half_up[:1, :8], half_down[:1, :8])
    steps.go(3)

    def near(k):
        at = slice(k * own, (k + 1) * own)
        return [mine[2][own:][at], first[own:][at], next_up[at], next_down[at]]

    up = tied(total(*near(1), widened(half_up, own, 0)), steps.x)
    down = total(*near(2), widened(half_down, own, half))
    ends = moved(up, FIRST_UP, back=True), moved(down, FIRST_DOWN, back=True)
    return total(*near(0), *ends)


def local(features, weight, tile_values, tile_cols, tile_live, cotangent):
    n_rows, n_rep = lax.axis_size("rows"), lax.axis_size("rep")
    rep = lax.axis_index("rep")
    node_dev, width = features.shape
    tile = tile_values.shape[2]
    own = node_dev // tile
    group_tiles = own * n_rep
    core = rep % 2
    plans = [layout(own, c) for c in range(2)]
    groups = [len(keys) for keys in plans[0]]
    table = np.zeros((2, 3, n_rep // 2, own), np.int32)
    for c, plan in enumerate(plans):
        for at, key in enumerate(sum(plan, [])):
            if key:
                table[(c, *key)] = at
    place = jnp.mod(tile_cols // group_tiles - lax.axis_index("rows") + 1, n_rows)
    inner = tile_cols % group_tiles
    owner = inner // own
    dy = jnp.mod(owner // 2 - rep // 2, n_rep // 2)
    key = (((owner % 2) * 3 + place) * (n_rep // 2) + dy) * own + inner % own
    hit = key[:, :, None] == jnp.arange(table.size, dtype=jnp.int32)
    at = jnp.sum(jnp.where(hit, jnp.asarray(table.reshape(-1)), 0), axis=2)
    idx = jnp.mod(owner + rep, 2) * sum(groups) + at
    cnt = jnp.sum(tile_live, axis=1)

    parts = gather(features, core)
    output, term, *grads = layer(idx, cnt, tile_values, parts, weight, cotangent, groups)
    steps = Steps(term, core)
    grad = scatter(grads[: len(groups)], grads[len(groups) :], own, core, steps)
    weight_grad = steps.whole()
    feature_grad = jnp.swapaxes(grad, 1, 2).reshape(node_dev, width)
    return (output, feature_grad, weight_grad)


def solution(mesh):
    placed = (
        P(("rows", "rep"), None),
        P(),
        P(("rows", "rep"), None, None, None),
        P(("rows", "rep"), None),
        P(("rows", "rep"), None),
        P(("rows", "rep"), None),
    )
    return jax.shard_map(
        local,
        mesh=mesh,
        in_specs=placed,
        out_specs=(P(("rows", "rep"), None), P(("rows", "rep"), None), P()),
        check_vma=False,
    )
```
